256 devices in a mesh: layer: 4 (over z_hi), tile: 64 (over y, z_lo, x, core).
Axes of the slice: x: 4, y: 4, z: 8 (z_hi: 4, z_lo: 2; z = z_hi * 2 + z_lo), core: 2. Of those that a mesh axis runs over, the one named last changes fastest.
Arguments:
- measured_slopes: float32 [6, 2, 768, 4096], P(None, None, 'tile'), may hold values from -18 to 18
- valid_mask: int32 [768, 4096], P('tile'), may hold values 0 or 1
- layer_offsets: int32 [6, 4, 2], replicated, may hold values from -8 to 8, as said below
- reg_weight: float32 [4], replicated, may hold values from 0.01 to 0.1
Outputs:
- layer_estimate: float32 [4, 768, 4096], P('layer', 'tile')
- residual: float32 [4, 768, 4096], P('layer', 'tile')
The draws below stay inside these ranges and needn't reach their ends.
Inputs may be any that keep to these rules, and one draw needn't show every extreme that they name: `layer_offsets`: every entry lies between -8 and 8; some entry equals 8 and some equals -8.
All inputs are finite; a program needn't handle non-finite values. No bound on the sum of `valid_mask` on one device may be relied on, other than what follows from the above.
Results may differ from the reference program's by a relative error of at most 0.0001.
Values sent between devices are 32-bit elements; how exact they have to be, the bound alone decides.
A program may use at most 64 MiB of HBM per device.

```python
import math
import jax
import jax.numpy as jnp
from jax import lax

COLS = 4096
DIRS = 6
HALO = 8
ITERS = 2
LAYERS = 4
NR = 768


def draw_measured_slopes(key, part):
    ramp = jnp.arange(NR, dtype=jnp.float32) / (NR - 1)
    base = jnp.clip(jax.random.normal(key, (DIRS, 2, NR, COLS), jnp.float32), -6.0, 6.0)
    scale = 1.0 + 2.0 * ramp
    return (base * scale[:, None]).astype(jnp.float32)


def draw_layer_offsets(key, part):
    drawn = jax.random.randint(key, (DIRS, LAYERS, 2), -HALO, HALO + 1)
    drawn = drawn.at[0, LAYERS - 1, :].set(HALO)
    drawn = drawn.at[1, LAYERS - 1, :].set(-HALO)
    return drawn.astype(jnp.int32)


def plant(values, own_key, low, high):
    dims = values.shape
    index_at = [jax.random.randint(jax.random.fold_in(own_key, axis), (), 0, dims[axis]) for axis in range(len(dims))]
    values = values.at[tuple(index_at)].set(low)
    longest = dims.index(max(dims))
    index_at[longest] = (index_at[longest] + 1) % dims[longest]
    return values.at[tuple(index_at)].set(high)


def setup_inputs(seed: int = 0) -> dict:
    arg_keys = jax.random.split(jax.random.key(seed), 5)
    return {
        "measured_slopes": draw_measured_slopes(jax.random.fold_in(arg_keys[4], 71), 0),
        "valid_mask": plant((jax.random.randint(arg_keys[1], (NR, COLS), 0, 8) < 7).astype(jnp.int32), jax.random.fold_in(arg_keys[1], 1), 0, 1),
        "layer_offsets": draw_layer_offsets(jax.random.fold_in(arg_keys[4], 71), 0),
        "reg_weight": jnp.clip(jnp.exp(jax.random.uniform(arg_keys[3], (LAYERS,), jnp.float32, math.log(0.01), math.log(0.1))), 0.01, 0.1),
    }


def shift_field(field, row_shift, col_shift):
    padded = jnp.pad(field, ((HALO, HALO), (HALO, HALO)))
    return lax.dynamic_slice(padded, (HALO + row_shift, HALO + col_shift), field.shape)


def fried_slopes(phase, maskf):
    padded = jnp.pad(phase, ((0, 1), (0, 1)))
    p00 = padded[:-1, :-1]
    p01 = padded[:-1, 1:]
    p10 = padded[1:, :-1]
    p11 = padded[1:, 1:]
    grad_x = 0.5 * (p01 - p00 + p11 - p10)
    grad_y = 0.5 * (p10 - p00 + p11 - p01)
    return maskf * grad_x, maskf * grad_y


def fried_adjoint(slope_x, slope_y):
    summed_x = slope_x + jnp.pad(slope_x, ((1, 0), (0, 0)))[:-1]
    summed_y = slope_y + jnp.pad(slope_y, ((0, 0), (1, 0)))[:, :-1]
    left_x = jnp.pad(summed_x, ((0, 0), (1, 0)))[:, :-1]
    upper_y = jnp.pad(summed_y, ((1, 0), (0, 0)))[:-1]
    return 0.5 * (left_x - summed_x + upper_y - summed_y)


def laplace(field):
    padded = jnp.pad(field, 1)
    return 4.0 * field - padded[:-2, 1:-1] - padded[2:, 1:-1] - padded[1:-1, :-2] - padded[1:-1, 2:]


def back_project(adjoints, layer_offsets, layer):
    total = jnp.zeros(adjoints[0].shape, jnp.float32)
    for direc in range(DIRS):
        total = total + shift_field(adjoints[direc], -layer_offsets[direc, layer, 0], -layer_offsets[direc, layer, 1])
    return total


def reference(measured_slopes, valid_mask, layer_offsets, reg_weight):
    maskf = valid_mask.astype(jnp.float32)

    def apply_operator(stack):
        adjoints = []
        for direc in range(DIRS):
            phase = jnp.zeros(stack.shape[1:], jnp.float32)
            for layer in range(LAYERS):
                phase = phase + shift_field(stack[layer], layer_offsets[direc, layer, 0], layer_offsets[direc, layer, 1])
            slope_x, slope_y = fried_slopes(phase, maskf)
            adjoints.append(fried_adjoint(slope_x, slope_y))
        result = []
        for layer in range(LAYERS):
            total = back_project(adjoints, layer_offsets, layer)
            result.append(total + reg_weight[layer] * laplace(laplace(stack[layer])))
        return jnp.stack(result)

    adjoints = [fried_adjoint(maskf * measured_slopes[direc, 0], maskf * measured_slopes[direc, 1]) for direc in range(DIRS)]
    right_side = jnp.stack([back_project(adjoints, layer_offsets, layer) for layer in range(LAYERS)])
    estimate = jnp.zeros_like(right_side)
    residual = right_side
    direction = right_side
    norm_now = jnp.sum(residual * residual)
    for step in range(ITERS):
        image = apply_operator(direction)
        alpha = norm_now / jnp.sum(direction * image)
        estimate = estimate + alpha * direction
        residual = residual - alpha * image
        norm_next = jnp.sum(residual * residual)
        direction = residual + (norm_next / norm_now) * direction
        norm_now = norm_next
    return estimate, residual
```

```python
import functools

import jax
import jax.numpy as jnp
from jax import lax
from jax.experimental import pallas as pl
from jax.experimental.pallas import tpu as pltpu
from jax.sharding import PartitionSpec as P

MESH = pl.DeviceIdType.MESH
F32 = jnp.float32
HALO = 8
MARGIN = 64
REACH = 17


def kernel(
    cfg,
    slopes_hbm, mask_hbm, off, reg,
    est_ref, res_ref,
    sl, mki, eb, q0, cb, sib, prv, nxt, ms, mb, x0, x1, pb, qb, lb, ya, tr, arsrc, ar1, ar2,
    in_sem, msend, mrecv, csend, crecv, hsend, hrecv, tsend, trecv, tlocal, asend, arecv,
):
    dirs, lays, tiles, rows, cols, nl = cfg
    two = 2 * rows
    width = cols // (2 * nl)
    at = width // 128
    nt = at + 1
    st = 2 * at + 2
    g1 = 16 if tiles % 16 == 0 else tiles
    hi = tiles // g1
    g2 = nl * hi
    lay = lax.axis_index("layer")
    t = lax.axis_index("tile")
    chip = lax.div(t, 2)
    h = lax.rem(t, 2)
    chips = tiles // 2
    has_prev = chip > 0
    has_next = chip < chips - 1
    prev0 = 2 * chip - 2
    next0 = 2 * chip + 2
    lane = lax.broadcasted_iota(jnp.int32, (8, 128), 1)
    sub = lax.broadcasted_iota(jnp.int32, (8, 128), 0)
    zero = jnp.zeros((8, 128), F32)

    def rdma(src, dst, ss, rs, dev):
        return pltpu.make_async_remote_copy(
            src_ref=src, dst_ref=dst, send_sem=ss, recv_sem=rs, device_id=dev, device_id_type=MESH
        )

    def wait_bytes(ref, sem):
        pltpu.make_async_copy(ref, ref, sem).wait()

    span = 2 * width

    def mask_in(first, count, at_tile):
        src, dst = pl.ds(pl.multiple_of(first, 128), count), pl.ds(128 * at_tile, count)
        return pltpu.make_async_copy(mask_hbm.at[:, src], mki.at[:, dst], in_sem.at[0])

    def slopes_in(first, count, at_tile):
        src, dst = pl.ds(pl.multiple_of(first, 128), count), pl.ds(128 * at_tile, count)
        return pltpu.make_async_copy(slopes_hbm.at[:, :, :, src], sl.at[:, :, :, dst], in_sem.at[1])

    def cases(act):
        @pl.when(lay == 0)
        def _():
            act(0, span + 128, 1)

        @pl.when(lay == nl - 1)
        def _():
            act(span * (nl - 1) - 128, span + 128, 0)

        @pl.when((lay > 0) & (lay < nl - 1))
        def _():
            act(span * lay - 128, span + 256, 0)

    cases(lambda *w: mask_in(*w).start())
    cases(lambda *w: slopes_in(*w).start())

    @pl.when(lay == 0)
    def _():
        mki[:, 0:128] = jnp.zeros((rows, 128), jnp.int32)
        sl[:, :, :, 0:128] = jnp.zeros((dirs, 2, rows, 128), F32)

    @pl.when(lay == nl - 1)
    def _():
        mki[:, 128 * (st - 1) :] = jnp.zeros((rows, 128), jnp.int32)
        sl[:, :, :, 128 * (st - 1) :] = jnp.zeros((dirs, 2, rows, 128), F32)

    prv[...] = jnp.zeros_like(prv)
    sib[...] = jnp.zeros_like(sib)
    mb[...] = jnp.zeros_like(mb)

    @pl.when(jnp.logical_not(has_next))
    def _():
        nxt[...] = jnp.zeros_like(nxt)

    x0[...] = jnp.zeros_like(x0)
    x1[...] = jnp.zeros_like(x1)

    barrier = pltpu.get_barrier_semaphore()

    def greet(dev):
        pl.semaphore_signal(barrier, inc=1, device_id=dev, device_id_type=MESH)

    other = 2 * chip + 1 - h
    greet((lay, other))

    @pl.when(has_prev)
    def _():
        greet((lay, prev0))
        greet((lay, prev0 + 1))

    @pl.when(has_next)
    def _():
        greet((lay, next0))
        greet((lay, next0 + 1))

    def greet_layers(d, c):
        there = lax.rem(lay + d, nl)
        greet((there, 2 * chip))
        greet((there, 2 * chip + 1))
        return c

    lax.fori_loop(1, nl, greet_layers, 0)
    low, high = lax.rem(t, g1), lax.div(t, g1)

    def member1(d):
        return (lay, high * g1 + lax.rem(low + d, g1))

    me2 = lay * hi + high

    def member2(d):
        index = lax.rem(me2 + d, g2)
        return (lax.div(index, hi), lax.rem(index, hi) * g1 + low)

    def greet1(d, c):
        greet(member1(d))
        return c

    def greet2(d, c):
        greet(member2(d))
        return c

    lax.fori_loop(1, g1, greet1, 0)
    lax.fori_loop(1, g2, greet2, 0)

    eb[...] = jnp.zeros_like(eb)
    q0[...] = jnp.zeros_like(q0)
    cb[:, :, :, 0:8, :] = jnp.zeros((2, lays, nt, 8, 128), F32)

    cases(lambda *w: mask_in(*w).wait())
    bands = [slice(0, 8), slice(8, rows)]
    for k in range(2):
        for band in bands:
            turned = [
                pltpu.roll(mki[band, 128 * j : 128 * j + 128].astype(F32), MARGIN + HALO, 1)
                for j in range(at * k, at * k + nt + 1)
            ]
            keep = lane[: band.stop - band.start] < MARGIN + HALO
            for j in range(nt):
                ms[k, j, band, :] = jnp.where(keep, turned[j], turned[j + 1])
    mine = HALO + 1 + rows * h
    for j in range(nt):
        mb[j, pl.ds(mine, rows), :] = ms[h, j, 0:rows, :]
    pl.semaphore_wait(
        barrier,
        1 + 2 * has_prev.astype(jnp.int32) + 2 * has_next.astype(jnp.int32) + 2 * (nl - 1) + (g1 - 1) + (g2 - 1),
    )

    def mask_sib():
        return rdma(
            ms.at[1 - h, :, pl.ds(0, rows)], mb.at[:, pl.ds(mine, rows)], msend.at[0], mrecv.at[0], (lay, other)
        )

    def mask_down(k):
        return rdma(
            ms.at[k, :, pl.ds(rows - HALO - 1, HALO + 1)], mb.at[:, pl.ds(0, HALO + 1)],
            msend.at[1 + k], mrecv.at[1], (lay, next0 + k),
        )

    def mask_up(k):
        return rdma(
            ms.at[k, :, pl.ds(0, HALO)], mb.at[:, pl.ds(HALO + 1 + two, HALO)],
            msend.at[1 + k], mrecv.at[2], (lay, prev0 + k),
        )

    sends_down = has_next & (h == 1)
    sends_up = has_prev & (h == 0)
    mask_sib().start()

    @pl.when(sends_down)
    def _():
        mask_down(0).start()
        mask_down(1).start()

    @pl.when(sends_up)
    def _():
        mask_up(0).start()
        mask_up(1).start()

    cases(lambda *w: slopes_in(*w).wait())
    first_row = rows * t

    def own_adjoint(g, c):
        for band in bands:
            for j in range(st):
                at_cols = slice(128 * j, 128 * j + 128)
                m = mki[band, at_cols].astype(F32)
                u = m * sl[g, 0, band, at_cols]
                w = m * sl[g, 1, band, at_cols]
                eb[0, j, 8 + band.start : 8 + band.stop, :] = u + w
                eb[1, j, 8 + band.start : 8 + band.stop, :] = u - w
        for rb in range(2):
            lo, up = 8 + 8 * rb, 7 + 8 * rb
            row_in = (first_row + 8 * rb + sub < rows * tiles).astype(F32)
            right = []
            for j in range(st):
                right.append(pltpu.roll(eb[0, j, up : up + 8, :] + eb[1, j, lo : lo + 8, :], 1, 1))
            for j in range(st):
                f = jnp.where(lane >= 1, right[j], right[max(j - 1, 0)])
                q = 0.5 * (f - eb[0, j, lo : lo + 8, :] - eb[1, j, up : up + 8, :])
                col_in = (span * lay - 128 + 128 * j + lane < cols).astype(F32)
                q0[g, j, 16 + 8 * rb : 24 + 8 * rb, :] = q * (row_in * col_in)
        return c

    lax.fori_loop(0, dirs, own_adjoint, 0)

    def part_sib(l):
        return rdma(
            cb.at[1 - h, l, :, pl.ds(8, rows + 17)], sib.at[l, :, pl.ds(8, rows + 17)],
            csend.at[l, 0], crecv.at[l, 0], (lay, other),
        )

    def part_down(l, k):
        return rdma(
            cb.at[k, l, :, pl.ds(16 + rows, 9)], prv.at[l, :, pl.ds(0, 9)],
            csend.at[l, 1 + k], crecv.at[l, 1], (lay, next0 + k),
        )

    def part_up(l, k):
        return rdma(
            cb.at[k, l, :, pl.ds(8, 8)], nxt.at[l], csend.at[l, 1 + k], crecv.at[l, 2], (lay, prev0 + k)
        )

    def parts(l, c):
        def block(rb, c):
            total = [[zero] * nt, [zero] * nt]
            for g in range(dirs):
                a, s = off[g, l, 0], MARGIN + off[g, l, 1]
                start = 8 + 8 * rb - a
                turned = [pltpu.roll(q0[g, j, pl.ds(start, 8), :], s, 1) for j in range(st)]
                keep = lane < s
                for k in range(2):
                    for j in range(nt):
                        total[k][j] = total[k][j] + jnp.where(keep, turned[at * k + j], turned[at * k + j + 1])
            for k in range(2):
                for j in range(nt):
                    cb[k, l, j, pl.ds(pl.multiple_of(8 + 8 * rb, 8), 8), :] = total[k][j]
            return c

        lax.fori_loop(0, 4, block, 0)
        part_sib(l).start()

        @pl.when(sends_down)
        def _():
            part_down(l, 0).start()
            part_down(l, 1).start()

        @pl.when(sends_up)
        def _():
            part_up(l, 0).start()
            part_up(l, 1).start()

        return c

    lax.fori_loop(0, lays, parts, 0)

    c0 = width * (2 * lay + h)
    xcol = [c0 - MARGIN + 128 * j + lane for j in range(nt)]
    x_in = [((v >= 0) & (v < cols)).astype(F32) for v in xcol]
    x_own = [((v >= c0) & (v < c0 + width)).astype(F32) for v in xcol]
    pcol = [c0 - MARGIN - HALO + 128 * j + lane for j in range(nt)]
    p_in = [((v >= 0) & (v < cols)).astype(F32) for v in pcol]
    p_own = [((v >= c0) & (v < c0 + width)).astype(F32) for v in pcol]
    chip_row = two * chip

    def row_inside(start):
        r = chip_row + start + sub
        return ((r >= 0) & (r < rows * tiles)).astype(F32)

    def halo_up(x, i, l):
        return rdma(
            x.at[l, :, pl.ds(24, REACH)], x.at[l, :, pl.ds(24 + two, REACH)],
            hsend.at[i, l, 0], hrecv.at[i, l, 0], (lay, prev0 + h),
        )

    def halo_down(x, i, l):
        return rdma(
            x.at[l, :, pl.ds(24 + two - REACH, REACH)], x.at[l, :, pl.ds(24 - REACH, REACH)],
            hsend.at[i, l, 1], hrecv.at[i, l, 1], (lay, next0 + h),
        )

    def send_halo(x, i, l):
        @pl.when(has_prev)
        def _():
            halo_up(x, i, l).start()

        @pl.when(has_next)
        def _():
            halo_down(x, i, l).start()

    def wait_halo(x, i, l):
        @pl.when(has_prev)
        def _():
            halo_down(x, i, l).wait_recv()

        @pl.when(has_next)
        def _():
            halo_up(x, i, l).wait_recv()

    def piece(i, l, half):
        src = ya.at[i, l, :, pl.ds(rows * half, rows)]
        dst = tr.at[i, pl.ds(at * (2 * lay + h), at), pl.ds(0, rows)]
        return src, dst

    def send_pieces(i, l):
        for half in range(2):
            src, dst = piece(i, l, half)
            here = (l == lay) & (half == h)

            @pl.when(here)
            def _():
                pltpu.make_async_copy(src, dst, tlocal.at[i]).start()

            @pl.when(jnp.logical_not(here))
            def _():
                rdma(src, dst, tsend.at[i], trecv.at[i], (l, 2 * chip + half)).start()

    def stage(i, l, rb, value):
        turned = [pltpu.roll(v, MARGIN, 1) for v in value]
        for k in range(at):
            ya[i, l, k, 8 * rb : 8 * rb + 8, :] = jnp.where(lane < MARGIN, turned[k], turned[k + 1])

    def finish_b(l, acc):
        part_sib(l).wait_recv()

        @pl.when(has_prev)
        def _():
            part_down(l, 0).wait_recv()

        @pl.when(has_next)
        def _():
            part_up(l, 0).wait_recv()

        for rb in range(two // 8):
            value = []
            for j in range(nt):
                v = cb[h, l, j, pl.ds(16 + 8 * rb - rows * h, 8), :]
                v = v + sib[l, j, pl.ds(16 + 8 * rb - rows * (1 - h), 8), :]
                if rb < 2:
                    v = v + prv[l, j, 8 * rb : 8 * rb + 8, :]
                if rb == two // 8 - 1:
                    v = v + nxt[l, j]
                v = v * x_in[j]
                acc = acc + x_own[j] * (v * v)
                x0[l, j, 24 + 8 * rb : 32 + 8 * rb, :] = v
                value.append(v)
            stage(0, l, rb, value)
        send_halo(x0, 0, l)
        send_pieces(0, l)
        return acc

    bb = lax.fori_loop(0, lays, finish_b, zero)

    mask_sib().wait_recv()

    @pl.when(has_prev)
    def _():
        mask_down(0).wait_recv()

    @pl.when(has_next)
    def _():
        mask_up(0).wait_recv()

    def beside(value):
        n = len(value)
        r = [pltpu.roll(v, 1, 1) for v in value]
        l = [pltpu.roll(v, 127, 1) for v in value]
        left = [jnp.where(lane >= 1, r[j], r[(j - 1) % n]) for j in range(n)]
        right = [jnp.where(lane < 127, l[j], l[(j + 1) % n]) for j in range(n)]
        return left, right

    def front(x, i):
        def smooth(l, acc):
            wait_halo(x, i, l)
            part = zero
            for rb in range(4):
                row = -1 + 8 * rb
                mid = [x[l, j, 24 + row : 32 + row, :] for j in range(nt)]
                left, right = beside(mid)
                inside = row_inside(row)
                own = ((row + sub >= 0) & (row + sub < two)).astype(F32)
                for j in range(nt):
                    v = 4.0 * mid[j] - x[l, j, 23 + row : 31 + row, :] - x[l, j, 25 + row : 33 + row, :]
                    v = (v - left[j] - right[j]) * (inside * x_in[j])
                    lb[l, j, 8 * rb : 8 * rb + 8, :] = v
                    part = part + (own * x_own[j]) * (v * v)
            return acc + reg[l] * part

        energy = lax.fori_loop(0, lays, smooth, zero)

        def project(g, acc):
            for rb in range(6):
                total = [zero] * nt
                for l in range(lays):
                    a, s = off[g, l, 0], HALO - off[g, l, 1]
                    start = 15 + 8 * rb + a
                    turned = [pltpu.roll(x[l, j, pl.ds(start, 8), :], s, 1) for j in range(nt)]
                    keep = lane >= s
                    total = [total[j] + jnp.where(keep, turned[j], turned[(j - 1) % nt]) for j in range(nt)]
                inside = row_inside(8 * rb - 9)
                total = [total[j] * (inside * p_in[j]) for j in range(nt)]
                turned = [pltpu.roll(v, 127, 1) for v in total]
                for j in range(nt):
                    pb[0, j, 8 * rb : 8 * rb + 8, :] = total[j]
                    pb[1, j, 8 * rb : 8 * rb + 8, :] = jnp.where(lane < 127, turned[j], turned[(j + 1) % nt])
            for rb in range(5):
                up, lo, dn = 8 * rb, 8 * rb + 1, 8 * rb + 2
                turned, rest = [], []
                inside = row_inside(8 * rb - 8)
                for j in range(nt):
                    m_lo, m_up = mb[j, lo : lo + 8, :], mb[j, up : up + 8, :]
                    p_lo, r_lo = pb[0, j, lo : lo + 8, :], pb[1, j, lo : lo + 8, :]
                    e1 = m_lo * (pb[1, j, dn : dn + 8, :] - p_lo)
                    e2 = m_lo * (r_lo - pb[0, j, dn : dn + 8, :])
                    e1_up = m_up * (r_lo - pb[0, j, up : up + 8, :])
                    e2_up = m_up * (pb[1, j, up : up + 8, :] - p_lo)
                    if 1 <= rb <= two // 8:
                        acc = acc + (0.5 * p_own[j]) * (e1 * e1 + e2 * e2)
                    turned.append(pltpu.roll(e1_up + e2, 1, 1))
                    rest.append(e1 + e2_up)
                for j in range(nt):
                    f = jnp.where(lane >= 1, turned[j], turned[(j - 1) % nt])
                    qb[g, j, 8 * rb : 8 * rb + 8, :] = (f - rest[j]) * (0.5 * inside * p_in[j])
            return acc

        return lax.fori_loop(0, dirs, project, energy)

    def back(i, x_next, first, last, acc):
        def layer(l, acc):
            for rb in range(two // 8):
                total = [zero] * nt
                for g in range(dirs):
                    a, s = off[g, l, 0], lax.rem(120 + off[g, l, 1], 128)
                    start = 8 + 8 * rb - a
                    turned = [pltpu.roll(qb[g, j, pl.ds(start, 8), :], s, 1) for j in range(nt)]
                    keep = lane < 120 + off[g, l, 1]
                    total = [total[j] + jnp.where(keep, turned[j], turned[(j + 1) % nt]) for j in range(nt)]
                lo = 8 * rb + 1
                mid = [lb[l, j, lo : lo + 8, :] for j in range(nt)]
                left, right = beside(mid)
                value = []
                for j in range(nt):
                    v = 4.0 * mid[j] - lb[l, j, lo - 1 : lo + 7, :] - lb[l, j, lo + 1 : lo + 9, :] - left[j] - right[j]
                    v = (total[j] + reg[l] * v) * x_in[j]
                    if x_next is not None:
                        acc = acc + x_own[j] * (v * v)
                        x_next[l, j, 24 + 8 * rb : 32 + 8 * rb, :] = v
                    value.append(v)
                stage(i, l, rb, value)
            if x_next is not None:
                send_halo(x_next, 1, l)
            send_pieces(i, l)
            return acc

        return lax.fori_loop(first, last, layer, acc)

    e0 = front(x0, 0)
    yy = back(1, x1, 0, lays, zero)
    e1 = front(x1, 1)

    def rowsum(v):
        return jnp.sum(v, axis=0, keepdims=True)

    packed = jnp.where(
        sub == 0, rowsum(bb), jnp.where(sub == 1, rowsum(e0), jnp.where(sub == 2, rowsum(yy), rowsum(e1)))
    )
    arsrc[0] = packed

    def exchange(stage_id, slots, count, member):
        def one(d, c):
            rdma(arsrc.at[stage_id], slots.at[count - 1 - d], asend.at[stage_id], arecv.at[stage_id], member(d)).start()
            return c

        lax.fori_loop(1, count, one, 0)

    exchange(0, ar1, g1, member1)
    half = (lays + 1) // 2
    back(2, None, 0, half, zero)
    wait_bytes(ar1, arecv.at[0])
    total = arsrc[0]
    for k in range(g1 - 1):
        total = total + ar1[k]
    arsrc[1] = total
    exchange(1, ar2, g2, member2)
    back(2, None, half, lays, zero)
    wait_bytes(ar2, arecv.at[1])
    total = arsrc[1]
    for k in range(g2 - 1):
        total = total + ar2[k]
    sums = jnp.sum(total, axis=1, keepdims=True)
    bb, e0, yy, e1 = (sums[k : k + 1] for k in range(4))
    a0 = bb / e0
    rr = a0 * a0 * yy - bb
    beta = rr / bb
    grown = 1.0 + beta
    a1 = rr / (grown * grown * e0 - 2.0 * a0 * grown * yy + a0 * a0 * e1)
    k0 = a0 + a1 * grown
    k1 = a0 * a1

    for i in range(3):
        wait_bytes(tr.at[i, pl.ds(0, at * (2 * nl - 1)), pl.ds(0, rows)], trecv.at[i])
        src, dst = piece(i, 0, 0)
        pltpu.make_async_copy(src, dst, tlocal.at[i]).wait()

    def write(ct, c):
        out = pl.ds(pl.multiple_of(128 * ct, 128), 128)
        b, y1, y2 = (tr[i, ct, 0:rows, :] for i in range(3))
        est_ref[0, :, out] = k0 * b - k1 * y1
        res_ref[0, :, out] = b - k0 * y1 + k1 * y2
        return c

    lax.fori_loop(0, cols // 128, write, 0, unroll=4)

    mask_sib().wait_send()

    @pl.when(sends_down)
    def _():
        mask_down(0).wait_send()
        mask_down(1).wait_send()

    @pl.when(sends_up)
    def _():
        mask_up(0).wait_send()
        mask_up(1).wait_send()

    def drain(l, c):
        part_sib(l).wait_send()

        @pl.when(sends_down)
        def _():
            part_down(l, 0).wait_send()
            part_down(l, 1).wait_send()

        @pl.when(sends_up)
        def _():
            part_up(l, 0).wait_send()
            part_up(l, 1).wait_send()

        for i, x in enumerate((x0, x1)):

            @pl.when(has_prev)
            def _():
                halo_up(x, i, l).wait_send()

            @pl.when(has_next)
            def _():
                halo_down(x, i, l).wait_send()

        return c

    lax.fori_loop(0, lays, drain, 0)
    for i in range(3):
        wait_bytes(tr.at[i, pl.ds(0, at * (2 * nl - 1)), pl.ds(0, rows)], tsend.at[i])
    wait_bytes(ar1, asend.at[0])
    wait_bytes(ar2, asend.at[1])


def per_device(shape, measured_slopes, valid_mask, layer_offsets, reg_weight):
    nl, tiles = shape
    dirs, _, rows, cols = measured_slopes.shape
    lays = layer_offsets.shape[1]
    width = cols // (2 * nl)
    at = width // 128
    nt, st = at + 1, 2 * at + 2
    g1 = 16 if tiles % 16 == 0 else tiles
    g2 = nl * tiles // g1
    vm = lambda *s: pltpu.VMEM(s, F32)
    dma = lambda *s: pltpu.SemaphoreType.DMA(s)
    out = jax.ShapeDtypeStruct((1, rows, cols), F32)
    return pl.pallas_call(
        functools.partial(kernel, (dirs, lays, tiles, rows, cols, nl)),
        out_shape=(out, out),
        in_specs=[pl.BlockSpec(memory_space=pl.ANY)] * 2 + [pl.BlockSpec(memory_space=pltpu.SMEM)] * 2,
        out_specs=(pl.BlockSpec(memory_space=pltpu.VMEM),) * 2,
        scratch_shapes=[
            vm(dirs, 2, rows, 128 * st),
            pltpu.VMEM((rows, 128 * st), jnp.int32),
            vm(2, st, 32, 128),
            vm(dirs, st, 48, 128),
            vm(2, lays, nt, 40, 128),
            vm(lays, nt, 40, 128),
            vm(lays, nt, 16, 128),
            vm(lays, nt, 8, 128),
            vm(2, nt, 16, 128),
            vm(nt, 56, 128),
            vm(lays, nt, 72, 128),
            vm(lays, nt, 72, 128),
            vm(2, nt, 48, 128),
            vm(dirs, nt, 40, 128),
            vm(lays, nt, 32, 128),
            vm(3, lays, at, 24, 128),
            vm(3, cols // 128, 16, 128),
            vm(2, 8, 128),
            vm(g1 - 1, 8, 128),
            vm(g2 - 1, 8, 128),
            dma(2), dma(3), dma(3), dma(lays, 3), dma(lays, 3), dma(2, lays, 2), dma(2, lays, 2),
            dma(3), dma(3), dma(3), dma(2), dma(2),
        ],
        compiler_params=pltpu.CompilerParams(
            collective_id=0, has_side_effects=True, vmem_limit_bytes=32 * 1024 * 1024
        ),
    )(measured_slopes, valid_mask, layer_offsets, reg_weight)


def solution(mesh):
    return jax.shard_map(
        functools.partial(per_device, (mesh.shape["layer"], mesh.shape["tile"])),
        mesh=mesh,
        in_specs=(P(None, None, "tile", None), P("tile", None), P(), P()),
        out_specs=(P("layer", "tile", None), P("layer", "tile", None)),
        check_vma=False,
    )
```

```python
import functools

import jax
import jax.numpy as jnp
from jax import lax
from jax.experimental import pallas as pl
from jax.experimental.pallas import tpu as pltpu
from jax.sharding import PartitionSpec as P

MESH = pl.DeviceIdType.MESH
F32 = jnp.float32
HALO = 8
MARGIN = 64
REACH = 17


def kernel(
    cfg,
    slopes_hbm, mask_hbm, off, reg,
    est_ref, res_ref,
    sl, mki, eb, q0, cb, sib, prv, nxt, ms, mb, x0, x1, pb, qb, lb, ya, tr, arsrc, ar1, ar2,
    in_sem, msend, mrecv, csend, crecv, hsend, hrecv, tsend, trecv, tlocal, asend, arecv,
):
    dirs, lays, tiles, rows, cols, nl = cfg
    two = 2 * rows
    width = cols // (2 * nl)
    at = width // 128
    nt = at + 1
    st = 2 * at + 2
    g1 = 16 if tiles % 16 == 0 else tiles
    hi = tiles // g1
    g2 = nl * hi
    lay = lax.axis_index("layer")
    t = lax.axis_index("tile")
    chip = lax.div(t, 2)
    h = lax.rem(t, 2)
    chips = tiles // 2
    has_prev = chip > 0
    has_next = chip < chips - 1
    prev0 = 2 * chip - 2
    next0 = 2 * chip + 2
    lane = lax.broadcasted_iota(jnp.int32, (8, 128), 1)
    sub = lax.broadcasted_iota(jnp.int32, (8, 128), 0)
    zero = jnp.zeros((8, 128), F32)

    def rdma(src, dst, ss, rs, dev):
        return pltpu.make_async_remote_copy(
            src_ref=src, dst_ref=dst, send_sem=ss, recv_sem=rs, device_id=dev, device_id_type=MESH
        )

    def wait_bytes(ref, sem):
        pltpu.make_async_copy(ref, ref, sem).wait()

    span = 2 * width

    def mask_in(first, count, at_tile):
        src, dst = pl.ds(pl.multiple_of(first, 128), count), pl.ds(128 * at_tile, count)
        return pltpu.make_async_copy(mask_hbm.at[:, src], mki.at[:, dst], in_sem.at[0])

    def slopes_in(first, count, at_tile):
        src, dst = pl.ds(lax.div(first, 64), count // 64), pl.ds(2 * at_tile, count // 64)

        def one(i, c):
            pltpu.make_async_copy(slopes_hbm.at[:, i, src], sl.at[:, dst, i], in_sem.at[1]).start()
            return c

        lax.fori_loop(0, rows, one, 0)

    def slopes_wait(first, count, at_tile):
        dst = sl.at[:, pl.ds(2 * at_tile, count // 64), pl.ds(0, rows)]
        pltpu.make_async_copy(dst, dst, in_sem.at[1]).wait()

    def cases(act):
        @pl.when(lay == 0)
        def _():
            act(0, span + 128, 1)

        @pl.when(lay == nl - 1)
        def _():
            act(span * (nl - 1) - 128, span + 128, 0)

        @pl.when((lay > 0) & (lay < nl - 1))
        def _():
            act(span * lay - 128, span + 256, 0)

    cases(lambda *w: mask_in(*w).start())
    cases(slopes_in)

    @pl.when(lay == 0)
    def _():
        mki[:, 0:128] = jnp.zeros((rows, 128), jnp.int32)
        sl[:, 0:2, 0:rows] = jnp.zeros((dirs, 2, rows, 128), F32)

    @pl.when(lay == nl - 1)
    def _():
        mki[:, 128 * (st - 1) :] = jnp.zeros((rows, 128), jnp.int32)
        sl[:, 2 * st - 2 :, 0:rows] = jnp.zeros((dirs, 2, rows, 128), F32)

    prv[...] = jnp.zeros_like(prv)
    sib[...] = jnp.zeros_like(sib)
    mb[...] = jnp.zeros_like(mb)

    @pl.when(jnp.logical_not(has_next))
    def _():
        nxt[...] = jnp.zeros_like(nxt)

    x0[...] = jnp.zeros_like(x0)
    x1[...] = jnp.zeros_like(x1)

    barrier = pltpu.get_barrier_semaphore()

    def greet(dev):
        pl.semaphore_signal(barrier, inc=1, device_id=dev, device_id_type=MESH)

    other = 2 * chip + 1 - h
    greet((lay, other))

    @pl.when(has_prev)
    def _():
        greet((lay, prev0))
        greet((lay, prev0 + 1))

    @pl.when(has_next)
    def _():
        greet((lay, next0))
        greet((lay, next0 + 1))

    def greet_layers(d, c):
        there = lax.rem(lay + d, nl)
        greet((there, 2 * chip))
        greet((there, 2 * chip + 1))
        return c

    lax.fori_loop(1, nl, greet_layers, 0)
    low, high = lax.rem(t, g1), lax.div(t, g1)

    def member1(d):
        return (lay, high * g1 + lax.rem(low + d, g1))

    me2 = lay * hi + high

    def member2(d):
        index = lax.rem(me2 + d, g2)
        return (lax.div(index, hi), lax.rem(index, hi) * g1 + low)

    def greet1(d, c):
        greet(member1(d))
        return c

    def greet2(d, c):
        greet(member2(d))
        return c

    lax.fori_loop(1, g1, greet1, 0)
    lax.fori_loop(1, g2, greet2, 0)

    eb[...] = jnp.zeros_like(eb)
    q0[...] = jnp.zeros_like(q0)
    cb[:, :, :, 0:8, :] = jnp.zeros((2, lays, nt, 8, 128), F32)

    cases(lambda *w: mask_in(*w).wait())
    bands = [slice(0, 8), slice(8, rows)]
    for k in range(2):
        for band in bands:
            turned = [
                pltpu.roll(mki[band, 128 * j : 128 * j + 128].astype(F32), MARGIN + HALO, 1)
                for j in range(at * k, at * k + nt + 1)
            ]
            keep = lane[: band.stop - band.start] < MARGIN + HALO
            for j in range(nt):
                ms[k, j, band, :] = jnp.where(keep, turned[j], turned[j + 1])
    mine = HALO + 1 + rows * h
    for j in range(nt):
        mb[j, pl.ds(mine, rows), :] = ms[h, j, 0:rows, :]
    pl.semaphore_wait(
        barrier,
        1 + 2 * has_prev.astype(jnp.int32) + 2 * has_next.astype(jnp.int32) + 2 * (nl - 1) + (g1 - 1) + (g2 - 1),
    )

    def mask_sib():
        return rdma(
            ms.at[1 - h, :, pl.ds(0, rows)], mb.at[:, pl.ds(mine, rows)], msend.at[0], mrecv.at[0], (lay, other)
        )

    def mask_down(k):
        return rdma(
            ms.at[k, :, pl.ds(rows - HALO - 1, HALO + 1)], mb.at[:, pl.ds(0, HALO + 1)],
            msend.at[1 + k], mrecv.at[1], (lay, next0 + k),
        )

    def mask_up(k):
        return rdma(
            ms.at[k, :, pl.ds(0, HALO)], mb.at[:, pl.ds(HALO + 1 + two, HALO)],
            msend.at[1 + k], mrecv.at[2], (lay, prev0 + k),
        )

    sends_down = has_next & (h == 1)
    sends_up = has_prev & (h == 0)
    mask_sib().start()

    @pl.when(sends_down)
    def _():
        mask_down(0).start()
        mask_down(1).start()

    @pl.when(sends_up)
    def _():
        mask_up(0).start()
        mask_up(1).start()

    cases(slopes_wait)
    first_row = rows * t

    def own_adjoint(g, c):
        for band in bands:
            for j in range(st):
                at_cols = slice(128 * j, 128 * j + 128)
                m = mki[band, at_cols].astype(F32)
                u = m * sl[g, 2 * j, band, :]
                w = m * sl[g, 2 * j + 1, band, :]
                eb[0, j, 8 + band.start : 8 + band.stop, :] = u + w
                eb[1, j, 8 + band.start : 8 + band.stop, :] = u - w
        for rb in range(2):
            lo, up = 8 + 8 * rb, 7 + 8 * rb
            row_in = (first_row + 8 * rb + sub < rows * tiles).astype(F32)
            right = []
            for j in range(st):
                right.append(pltpu.roll(eb[0, j, up : up + 8, :] + eb[1, j, lo : lo + 8, :], 1, 1))
            for j in range(st):
                f = jnp.where(lane >= 1, right[j], right[max(j - 1, 0)])
                q = 0.5 * (f - eb[0, j, lo : lo + 8, :] - eb[1, j, up : up + 8, :])
                col_in = (span * lay - 128 + 128 * j + lane < cols).astype(F32)
                q0[g, j, 16 + 8 * rb : 24 + 8 * rb, :] = q * (row_in * col_in)
        return c

    lax.fori_loop(0, dirs, own_adjoint, 0)

    def part_sib(l):
        return rdma(
            cb.at[1 - h, l, :, pl.ds(8, rows + 17)], sib.at[l, :, pl.ds(8, rows + 17)],
            csend.at[l, 0], crecv.at[l, 0], (lay, other),
        )

    def part_down(l, k):
        return rdma(
            cb.at[k, l, :, pl.ds(16 + rows, 9)], prv.at[l, :, pl.ds(0, 9)],
            csend.at[l, 1 + k], crecv.at[l, 1], (lay, next0 + k),
        )

    def part_up(l, k):
        return rdma(
            cb.at[k, l, :, pl.ds(8, 8)], nxt.at[l], csend.at[l, 1 + k], crecv.at[l, 2], (lay, prev0 + k)
        )

    def parts(l, c):
        def block(rb, c):
            total = [[zero] * nt, [zero] * nt]
            for g in range(dirs):
                a, s = off[l, 0, g], MARGIN + off[l, 1, g]
                start = 8 + 8 * rb - a
                turned = [pltpu.roll(q0[g, j, pl.ds(start, 8), :], s, 1) for j in range(st)]
                keep = lane < s
                for k in range(2):
                    for j in range(nt):
                        total[k][j] = total[k][j] + jnp.where(keep, turned[at * k + j], turned[at * k + j + 1])
            for k in range(2):
                for j in range(nt):
                    cb[k, l, j, pl.ds(pl.multiple_of(8 + 8 * rb, 8), 8), :] = total[k][j]
            return c

        lax.fori_loop(0, 4, block, 0)
        part_sib(l).start()

        @pl.when(sends_down)
        def _():
            part_down(l, 0).start()
            part_down(l, 1).start()

        @pl.when(sends_up)
        def _():
            part_up(l, 0).start()
            part_up(l, 1).start()

        return c

    lax.fori_loop(0, lays, parts, 0)

    c0 = width * (2 * lay + h)
    xcol = [c0 - MARGIN + 128 * j + lane for j in range(nt)]
    x_in = [((v >= 0) & (v < cols)).astype(F32) for v in xcol]
    x_own = [((v >= c0) & (v < c0 + width)).astype(F32) for v in xcol]
    pcol = [c0 - MARGIN - HALO + 128 * j + lane for j in range(nt)]
    p_in = [((v >= 0) & (v < cols)).astype(F32) for v in pcol]
    p_own = [((v >= c0) & (v < c0 + width)).astype(F32) for v in pcol]
    chip_row = two * chip

    def row_inside(start):
        r = chip_row + start + sub
        return ((r >= 0) & (r < rows * tiles)).astype(F32)

    def halo_up(x, i, l):
        return rdma(
            x.at[l, :, pl.ds(24, REACH)], x.at[l, :, pl.ds(24 + two, REACH)],
            hsend.at[i, l, 0], hrecv.at[i, l, 0], (lay, prev0 + h),
        )

    def halo_down(x, i, l):
        return rdma(
            x.at[l, :, pl.ds(24 + two - REACH, REACH)], x.at[l, :, pl.ds(24 - REACH, REACH)],
            hsend.at[i, l, 1], hrecv.at[i, l, 1], (lay, next0 + h),
        )

    def send_halo(x, i, l):
        @pl.when(has_prev)
        def _():
            halo_up(x, i, l).start()

        @pl.when(has_next)
        def _():
            halo_down(x, i, l).start()

    def wait_halo(x, i, l):
        @pl.when(has_prev)
        def _():
            halo_down(x, i, l).wait_recv()

        @pl.when(has_next)
        def _():
            halo_up(x, i, l).wait_recv()

    def piece(i, l, half):
        src = ya.at[i, l, pl.ds(at * rows * half, at * rows)].reshape(rows, at, 128)
        dst = tr.at[i, :, pl.ds(at * (2 * lay + h), at)]
        return src, dst

    def send_pieces(i, l):
        for half in range(2):
            src, dst = piece(i, l, half)
            here = (l == lay) & (half == h)

            @pl.when(here)
            def _():
                pltpu.make_async_copy(src, dst, tlocal.at[i]).start()

            @pl.when(jnp.logical_not(here))
            def _():
                rdma(src, dst, tsend.at[i], trecv.at[i], (l, 2 * chip + half)).start()

    def stage(i, l, rb, value):
        turned = [pltpu.roll(v, MARGIN, 1) for v in value]
        for k in range(at):
            ya[i, l, pl.ds(at * 8 * rb + k, 8, stride=at), :] = jnp.where(lane < MARGIN, turned[k], turned[k + 1])

    def finish_b(l, acc):
        part_sib(l).wait_recv()

        @pl.when(has_prev)
        def _():
            part_down(l, 0).wait_recv()

        @pl.when(has_next)
        def _():
            part_up(l, 0).wait_recv()

        for rb in range(two // 8):
            value = []
            for j in range(nt):
                v = cb[h, l, j, pl.ds(16 + 8 * rb - rows * h, 8), :]
                v = v + sib[l, j, pl.ds(16 + 8 * rb - rows * (1 - h), 8), :]
                if rb < 2:
                    v = v + prv[l, j, 8 * rb : 8 * rb + 8, :]
                if rb == two // 8 - 1:
                    v = v + nxt[l, j]
                v = v * x_in[j]
                acc = acc + x_own[j] * (v * v)
                x0[l, j, 24 + 8 * rb : 32 + 8 * rb, :] = v
                value.append(v)
            stage(0, l, rb, value)
        send_halo(x0, 0, l)
        send_pieces(0, l)
        return acc

    bb = lax.fori_loop(0, lays, finish_b, zero)

    mask_sib().wait_recv()

    @pl.when(has_prev)
    def _():
        mask_down(0).wait_recv()

    @pl.when(has_next)
    def _():
        mask_up(0).wait_recv()

    def beside(value):
        n = len(value)
        r = [pltpu.roll(v, 1, 1) for v in value]
        l = [pltpu.roll(v, 127, 1) for v in value]
        left = [jnp.where(lane >= 1, r[j], r[(j - 1) % n]) for j in range(n)]
        right = [jnp.where(lane < 127, l[j], l[(j + 1) % n]) for j in range(n)]
        return left, right

    def front(x, i):
        def smooth(l, acc):
            wait_halo(x, i, l)
            part = zero
            for rb in range(4):
                row = -1 + 8 * rb
                mid = [x[l, j, 24 + row : 32 + row, :] for j in range(nt)]
                left, right = beside(mid)
                inside = row_inside(row)
                own = ((row + sub >= 0) & (row + sub < two)).astype(F32)
                for j in range(nt):
                    v = 4.0 * mid[j] - x[l, j, 23 + row : 31 + row, :] - x[l, j, 25 + row : 33 + row, :]
                    v = (v - left[j] - right[j]) * (inside * x_in[j])
                    lb[l, j, 8 * rb : 8 * rb + 8, :] = v
                    part = part + (own * x_own[j]) * (v * v)
            return acc + reg[l] * part

        energy = lax.fori_loop(0, lays, smooth, zero)

        def project(g, acc):
            for rb in range(6):
                total = [zero] * nt
                for l in range(lays):
                    a, s = off[l, 0, g], HALO - off[l, 1, g]
                    start = 15 + 8 * rb + a
                    turned = [pltpu.roll(x[l, j, pl.ds(start, 8), :], s, 1) for j in range(nt)]
                    keep = lane >= s
                    total = [total[j] + jnp.where(keep, turned[j], turned[(j - 1) % nt]) for j in range(nt)]
                inside = row_inside(8 * rb - 9)
                total = [total[j] * (inside * p_in[j]) for j in range(nt)]
                turned = [pltpu.roll(v, 127, 1) for v in total]
                for j in range(nt):
                    pb[0, j, 8 * rb : 8 * rb + 8, :] = total[j]
                    pb[1, j, 8 * rb : 8 * rb + 8, :] = jnp.where(lane < 127, turned[j], turned[(j + 1) % nt])
            for rb in range(5):
                up, lo, dn = 8 * rb, 8 * rb + 1, 8 * rb + 2
                turned, rest = [], []
                inside = row_inside(8 * rb - 8)
                for j in range(nt):
                    m_lo, m_up = mb[j, lo : lo + 8, :], mb[j, up : up + 8, :]
                    p_lo, r_lo = pb[0, j, lo : lo + 8, :], pb[1, j, lo : lo + 8, :]
                    e1 = m_lo * (pb[1, j, dn : dn + 8, :] - p_lo)
                    e2 = m_lo * (r_lo - pb[0, j, dn : dn + 8, :])
                    e1_up = m_up * (r_lo - pb[0, j, up : up + 8, :])
                    e2_up = m_up * (pb[1, j, up : up + 8, :] - p_lo)
                    if 1 <= rb <= two // 8:
                        acc = acc + (0.5 * p_own[j]) * (e1 * e1 + e2 * e2)
                    turned.append(pltpu.roll(e1_up + e2, 1, 1))
                    rest.append(e1 + e2_up)
                for j in range(nt):
                    f = jnp.where(lane >= 1, turned[j], turned[(j - 1) % nt])
                    qb[g, j, 8 * rb : 8 * rb + 8, :] = (f - rest[j]) * (0.5 * inside * p_in[j])
            return acc

        return lax.fori_loop(0, dirs, project, energy)

    def back(i, x_next, first, last, acc):
        def layer(l, acc):
            for rb in range(two // 8):
                total = [zero] * nt
                for g in range(dirs):
                    a, s = off[l, 0, g], lax.rem(120 + off[l, 1, g], 128)
                    start = 8 + 8 * rb - a
                    turned = [pltpu.roll(qb[g, j, pl.ds(start, 8), :], s, 1) for j in range(nt)]
                    keep = lane < 120 + off[l, 1, g]
                    total = [total[j] + jnp.where(keep, turned[j], turned[(j + 1) % nt]) for j in range(nt)]
                lo = 8 * rb + 1
                mid = [lb[l, j, lo : lo + 8, :] for j in range(nt)]
                left, right = beside(mid)
                value = []
                for j in range(nt):
                    v = 4.0 * mid[j] - lb[l, j, lo - 1 : lo + 7, :] - lb[l, j, lo + 1 : lo + 9, :] - left[j] - right[j]
                    v = (total[j] + reg[l] * v) * x_in[j]
                    if x_next is not None:
                        acc = acc + x_own[j] * (v * v)
                        x_next[l, j, 24 + 8 * rb : 32 + 8 * rb, :] = v
                    value.append(v)
                stage(i, l, rb, value)
            if x_next is not None:
                send_halo(x_next, 1, l)
            send_pieces(i, l)
            return acc

        return lax.fori_loop(first, last, layer, acc)

    e0 = front(x0, 0)
    yy = back(1, x1, 0, lays, zero)
    e1 = front(x1, 1)

    def rowsum(v):
        return jnp.sum(v, axis=0, keepdims=True)

    packed = jnp.where(
        sub == 0, rowsum(bb), jnp.where(sub == 1, rowsum(e0), jnp.where(sub == 2, rowsum(yy), rowsum(e1)))
    )
    arsrc[0] = packed

    def exchange(stage_id, slots, count, member):
        def one(d, c):
            rdma(arsrc.at[stage_id], slots.at[count - 1 - d], asend.at[stage_id], arecv.at[stage_id], member(d)).start()
            return c

        lax.fori_loop(1, count, one, 0)

    exchange(0, ar1, g1, member1)
    half = (lays + 1) // 2
    back(2, None, 0, half, zero)
    wait_bytes(ar1, arecv.at[0])
    total = arsrc[0]
    for k in range(g1 - 1):
        total = total + ar1[k]
    arsrc[1] = total
    exchange(1, ar2, g2, member2)
    back(2, None, half, lays, zero)
    wait_bytes(ar2, arecv.at[1])
    total = arsrc[1]
    for k in range(g2 - 1):
        total = total + ar2[k]
    sums = jnp.sum(total, axis=1, keepdims=True)
    bb, e0, yy, e1 = (sums[k : k + 1] for k in range(4))
    a0 = bb / e0
    rr = a0 * a0 * yy - bb
    beta = rr / bb
    grown = 1.0 + beta
    a1 = rr / (grown * grown * e0 - 2.0 * a0 * grown * yy + a0 * a0 * e1)
    k0 = a0 + a1 * grown
    k1 = a0 * a1

    for i in range(3):
        wait_bytes(tr.at[i, :, pl.ds(0, at * (2 * nl - 1))], trecv.at[i])
        src, dst = piece(i, 0, 0)
        pltpu.make_async_copy(src, dst, tlocal.at[i]).wait()

    def write(r, c):
        for ct in range(0, cols // 128, 8):
            b, y1, y2 = (tr[i, r, ct : ct + 8, :] for i in range(3))
            est_ref[r, ct : ct + 8, :] = k0 * b - k1 * y1
            res_ref[r, ct : ct + 8, :] = b - k0 * y1 + k1 * y2
        return c

    lax.fori_loop(0, rows, write, 0, unroll=2)

    mask_sib().wait_send()

    @pl.when(sends_down)
    def _():
        mask_down(0).wait_send()
        mask_down(1).wait_send()

    @pl.when(sends_up)
    def _():
        mask_up(0).wait_send()
        mask_up(1).wait_send()

    def drain(l, c):
        part_sib(l).wait_send()

        @pl.when(sends_down)
        def _():
            part_down(l, 0).wait_send()
            part_down(l, 1).wait_send()

        @pl.when(sends_up)
        def _():
            part_up(l, 0).wait_send()
            part_up(l, 1).wait_send()

        for i, x in enumerate((x0, x1)):

            @pl.when(has_prev)
            def _():
                halo_up(x, i, l).wait_send()

            @pl.when(has_next)
            def _():
                halo_down(x, i, l).wait_send()

        return c

    lax.fori_loop(0, lays, drain, 0)
    for i in range(3):
        wait_bytes(tr.at[i, :, pl.ds(0, at * (2 * nl - 1))], tsend.at[i])
    wait_bytes(ar1, asend.at[0])
    wait_bytes(ar2, asend.at[1])


def per_device(shape, measured_slopes, valid_mask, layer_offsets, reg_weight):
    nl, tiles = shape
    dirs, _, rows, cols = measured_slopes.shape
    lays = layer_offsets.shape[1]
    width = cols // (2 * nl)
    at = width // 128
    nt, st = at + 1, 2 * at + 2
    g1 = 16 if tiles % 16 == 0 else tiles
    g2 = nl * tiles // g1
    vm = lambda *s: pltpu.VMEM(s, F32)
    dma = lambda *s: pltpu.SemaphoreType.DMA(s)
    out = jax.ShapeDtypeStruct((rows, cols // 128, 128), F32)
    slopes = measured_slopes.reshape(dirs, 2, rows, cols // 128, 128).transpose(0, 2, 3, 1, 4)
    slopes = slopes.reshape(dirs, rows, cols // 64, 128)
    est, res = pl.pallas_call(
        functools.partial(kernel, (dirs, lays, tiles, rows, cols, nl)),
        out_shape=(out, out),
        in_specs=[pl.BlockSpec(memory_space=pltpu.HBM)] * 2 + [pl.BlockSpec(memory_space=pltpu.SMEM)] * 2,
        out_specs=(pl.BlockSpec(memory_space=pltpu.VMEM),) * 2,
        scratch_shapes=[
            vm(dirs, 2 * st, rows + 4, 128),
            pltpu.VMEM((rows, 128 * st), jnp.int32),
            vm(2, st, 32, 128),
            vm(dirs, st, 48, 128),
            vm(2, lays, nt, 40, 128),
            vm(lays, nt, 40, 128),
            vm(lays, nt, 16, 128),
            vm(lays, nt, 8, 128),
            vm(2, nt, 16, 128),
            vm(nt, 56, 128),
            vm(lays, nt, 72, 128),
            vm(lays, nt, 72, 128),
            vm(2, nt, 48, 128),
            vm(dirs, nt, 40, 128),
            vm(lays, nt, 32, 128),
            vm(3, lays, at * 2 * rows, 128),
            vm(3, rows, cols // 128, 128),
            vm(2, 8, 128),
            vm(g1 - 1, 8, 128),
            vm(g2 - 1, 8, 128),
            dma(2), dma(3), dma(3), dma(lays, 3), dma(lays, 3), dma(2, lays, 2), dma(2, lays, 2),
            dma(3), dma(3), dma(3), dma(2), dma(2),
        ],
        compiler_params=pltpu.CompilerParams(
            collective_id=0, has_side_effects=True, vmem_limit_bytes=56 * 1024 * 1024
        ),
    )(slopes, valid_mask, layer_offsets.transpose(1, 2, 0), reg_weight)
    return est.reshape(1, rows, cols), res.reshape(1, rows, cols)


def solution(mesh):
    return jax.shard_map(
        functools.partial(per_device, (mesh.shape["layer"], mesh.shape["tile"])),
        mesh=mesh,
        in_specs=(P(None, None, "tile", None), P("tile", None), P(), P()),
        out_specs=(P("layer", "tile", None), P("layer", "tile", None)),
        check_vma=False,
    )
```

```python
import functools

import jax
import jax.numpy as jnp
from jax import lax
from jax.experimental import pallas as pl
from jax.experimental.pallas import tpu as pltpu
from jax.sharding import PartitionSpec as P

MESH = pl.DeviceIdType.MESH
F32 = jnp.float32
HALO = 8
MARGIN = 64
REACH = 17


def kernel(
    cfg,
    slopes_hbm, mask_hbm, off, reg,
    b_out, y1_out, y2_out, k0_ref, k1_ref,
    sl, mki, eb, q0, cb, sib, prv, nxt, ms, mb, x0, x1, pb, qb, lb, ya, arsrc, ar1, ar2,
    in_sem, msend, mrecv, csend, crecv, hsend, hrecv, tsend, trecv, tlocal, asend, arecv,
):
    dirs, lays, tiles, rows, cols, nl = cfg
    two = 2 * rows
    outs = (b_out, y1_out, y2_out)
    width = cols // (2 * nl)
    at = width // 128
    nt = at + 1
    st = 2 * at + 2
    zs, xs = (2, 4) if tiles % 16 == 0 else (1, tiles // 2)
    g1 = nl * zs * 2
    g2 = tiles // (zs * 2)
    lay = lax.axis_index("layer")
    t = lax.axis_index("tile")
    chip = lax.div(t, 2)
    h = lax.rem(t, 2)
    chips = tiles // 2
    has_prev = chip > 0
    has_next = chip < chips - 1
    prev0 = 2 * chip - 2
    next0 = 2 * chip + 2
    lane = lax.broadcasted_iota(jnp.int32, (8, 128), 1)
    sub = lax.broadcasted_iota(jnp.int32, (8, 128), 0)
    zero = jnp.zeros((8, 128), F32)

    def rdma(src, dst, ss, rs, dev):
        return pltpu.make_async_remote_copy(
            src_ref=src, dst_ref=dst, send_sem=ss, recv_sem=rs, device_id=dev, device_id_type=MESH
        )

    def wait_bytes(ref, sem):
        pltpu.make_async_copy(ref, ref, sem).wait()

    span = 2 * width

    def mask_in(first, count, at_tile):
        src, dst = pl.ds(pl.multiple_of(first, 128), count), pl.ds(128 * at_tile, count)
        return pltpu.make_async_copy(mask_hbm.at[:, src], mki.at[:, dst], in_sem.at[0])

    def slopes_in(first, count, at_tile):
        src, dst = pl.ds(lax.div(first, 64), count // 64), pl.ds(2 * at_tile, count // 64)

        def one(i, c):
            pltpu.make_async_copy(slopes_hbm.at[:, i, src], sl.at[:, dst, i], in_sem.at[1]).start()
            return c

        lax.fori_loop(0, rows, one, 0)

    def slopes_wait(first, count, at_tile):
        dst = sl.at[:, pl.ds(2 * at_tile, count // 64), pl.ds(0, rows)]
        pltpu.make_async_copy(dst, dst, in_sem.at[1]).wait()

    def cases(act):
        @pl.when(lay == 0)
        def _():
            act(0, span + 128, 1)

        @pl.when(lay == nl - 1)
        def _():
            act(span * (nl - 1) - 128, span + 128, 0)

        @pl.when((lay > 0) & (lay < nl - 1))
        def _():
            act(span * lay - 128, span + 256, 0)

    cases(lambda *w: mask_in(*w).start())
    cases(slopes_in)

    @pl.when(lay == 0)
    def _():
        mki[:, 0:128] = jnp.zeros((rows, 128), jnp.int32)
        sl[:, 0:2, 0:rows] = jnp.zeros((dirs, 2, rows, 128), F32)

    @pl.when(lay == nl - 1)
    def _():
        mki[:, 128 * (st - 1) :] = jnp.zeros((rows, 128), jnp.int32)
        sl[:, 2 * st - 2 :, 0:rows] = jnp.zeros((dirs, 2, rows, 128), F32)

    prv[...] = jnp.zeros_like(prv)
    sib[...] = jnp.zeros_like(sib)
    mb[...] = jnp.zeros_like(mb)

    @pl.when(jnp.logical_not(has_next))
    def _():
        nxt[...] = jnp.zeros_like(nxt)

    x0[...] = jnp.zeros_like(x0)
    x1[...] = jnp.zeros_like(x1)

    barrier = pltpu.get_barrier_semaphore()

    def greet(dev):
        pl.semaphore_signal(barrier, inc=1, device_id=dev, device_id_type=MESH)

    other = 2 * chip + 1 - h
    greet((lay, other))

    @pl.when(has_prev)
    def _():
        greet((lay, prev0))
        greet((lay, prev0 + 1))

    @pl.when(has_next)
    def _():
        greet((lay, next0))
        greet((lay, next0 + 1))

    def greet_layers(d, c):
        there = lax.rem(lay + d, nl)
        greet((there, 2 * chip))
        greet((there, 2 * chip + 1))
        return c

    lax.fori_loop(1, nl, greet_layers, 0)
    tx, tz, ty = lax.rem(chip, xs), lax.rem(lax.div(chip, xs), zs), lax.div(chip, xs * zs)
    me1 = (lay * zs + tz) * 2 + h
    me2 = ty * xs + tx

    def tile_at(y, z, x, core):
        return ((y * zs + z) * xs + x) * 2 + core

    def member1(d):
        index = lax.rem(me1 + d, g1)
        there = lax.div(index, 2 * zs)
        return (there, tile_at(ty, lax.rem(lax.div(index, 2), zs), tx, lax.rem(index, 2)))

    def member2(d):
        index = lax.rem(me2 + d, g2)
        return (lay, tile_at(lax.div(index, xs), tz, lax.rem(index, xs), h))

    def greet1(d, c):
        greet(member1(d))
        return c

    def greet2(d, c):
        greet(member2(d))
        return c

    lax.fori_loop(1, g1, greet1, 0)
    lax.fori_loop(1, g2, greet2, 0)

    eb[...] = jnp.zeros_like(eb)
    q0[...] = jnp.zeros_like(q0)
    cb[:, :, :, 0:8, :] = jnp.zeros((2, lays, nt, 8, 128), F32)

    cases(lambda *w: mask_in(*w).wait())
    bands = [slice(0, 8), slice(8, rows)]
    for k in range(2):
        for band in bands:
            turned = [
                pltpu.roll(mki[band, 128 * j : 128 * j + 128].astype(F32), MARGIN + HALO, 1)
                for j in range(at * k, at * k + nt + 1)
            ]
            keep = lane[: band.stop - band.start] < MARGIN + HALO
            for j in range(nt):
                ms[k, j, band, :] = jnp.where(keep, turned[j], turned[j + 1])
    mine = HALO + 1 + rows * h
    for j in range(nt):
        mb[j, pl.ds(mine, rows), :] = ms[h, j, 0:rows, :]
    pl.semaphore_wait(
        barrier,
        1 + 2 * has_prev.astype(jnp.int32) + 2 * has_next.astype(jnp.int32) + 2 * (nl - 1) + (g1 - 1) + (g2 - 1),
    )

    def mask_sib():
        return rdma(
            ms.at[1 - h, :, pl.ds(0, rows)], mb.at[:, pl.ds(mine, rows)], msend.at[0], mrecv.at[0], (lay, other)
        )

    def mask_down(k):
        return rdma(
            ms.at[k, :, pl.ds(rows - HALO - 1, HALO + 1)], mb.at[:, pl.ds(0, HALO + 1)],
            msend.at[1 + k], mrecv.at[1], (lay, next0 + k),
        )

    def mask_up(k):
        return rdma(
            ms.at[k, :, pl.ds(0, HALO)], mb.at[:, pl.ds(HALO + 1 + two, HALO)],
            msend.at[1 + k], mrecv.at[2], (lay, prev0 + k),
        )

    sends_down = has_next & (h == 1)
    sends_up = has_prev & (h == 0)
    mask_sib().start()

    @pl.when(sends_down)
    def _():
        mask_down(0).start()
        mask_down(1).start()

    @pl.when(sends_up)
    def _():
        mask_up(0).start()
        mask_up(1).start()

    cases(slopes_wait)
    first_row = rows * t

    def own_adjoint(g, c):
        for band in bands:
            for j in range(st):
                at_cols = slice(128 * j, 128 * j + 128)
                m = mki[band, at_cols].astype(F32)
                u = m * sl[g, 2 * j, band, :]
                w = m * sl[g, 2 * j + 1, band, :]
                eb[0, j, 8 + band.start : 8 + band.stop, :] = u + w
                eb[1, j, 8 + band.start : 8 + band.stop, :] = u - w
        for rb in range(2):
            lo, up = 8 + 8 * rb, 7 + 8 * rb
            row_in = (first_row + 8 * rb + sub < rows * tiles).astype(F32)
            right = []
            for j in range(st):
                right.append(pltpu.roll(eb[0, j, up : up + 8, :] + eb[1, j, lo : lo + 8, :], 1, 1))
            for j in range(st):
                f = jnp.where(lane >= 1, right[j], right[max(j - 1, 0)])
                q = 0.5 * (f - eb[0, j, lo : lo + 8, :] - eb[1, j, up : up + 8, :])
                col_in = (span * lay - 128 + 128 * j + lane < cols).astype(F32)
                q0[g, j, 16 + 8 * rb : 24 + 8 * rb, :] = q * (row_in * col_in)
        return c

    lax.fori_loop(0, dirs, own_adjoint, 0)

    def part_sib(l):
        return rdma(
            cb.at[1 - h, l, :, pl.ds(8, rows + 17)], sib.at[l, :, pl.ds(8, rows + 17)],
            csend.at[l, 0], crecv.at[l, 0], (lay, other),
        )

    def part_down(l, k):
        return rdma(
            cb.at[k, l, :, pl.ds(16 + rows, 9)], prv.at[l, :, pl.ds(0, 9)],
            csend.at[l, 1 + k], crecv.at[l, 1], (lay, next0 + k),
        )

    def part_up(l, k):
        return rdma(
            cb.at[k, l, :, pl.ds(8, 8)], nxt.at[l], csend.at[l, 1 + k], crecv.at[l, 2], (lay, prev0 + k)
        )

    def parts(l, c):
        def block(rb, c):
            total = [[zero] * nt, [zero] * nt]
            for g in range(dirs):
                a, s = off[l, 0, g], MARGIN + off[l, 1, g]
                start = 8 + 8 * rb - a
                turned = [pltpu.roll(q0[g, j, pl.ds(start, 8), :], s, 1) for j in range(st)]
                keep = lane < s
                for k in range(2):
                    for j in range(nt):
                        total[k][j] = total[k][j] + jnp.where(keep, turned[at * k + j], turned[at * k + j + 1])
            for k in range(2):
                for j in range(nt):
                    cb[k, l, j, pl.ds(pl.multiple_of(8 + 8 * rb, 8), 8), :] = total[k][j]
            return c

        lax.fori_loop(0, 4, block, 0)
        part_sib(l).start()

        @pl.when(sends_down)
        def _():
            part_down(l, 0).start()
            part_down(l, 1).start()

        @pl.when(sends_up)
        def _():
            part_up(l, 0).start()
            part_up(l, 1).start()

        return c

    lax.fori_loop(0, lays, parts, 0)

    c0 = width * (2 * lay + h)
    xcol = [c0 - MARGIN + 128 * j + lane for j in range(nt)]
    x_in = [((v >= 0) & (v < cols)).astype(F32) for v in xcol]
    x_own = [((v >= c0) & (v < c0 + width)).astype(F32) for v in xcol]
    pcol = [c0 - MARGIN - HALO + 128 * j + lane for j in range(nt)]
    p_in = [((v >= 0) & (v < cols)).astype(F32) for v in pcol]
    p_own = [((v >= c0) & (v < c0 + width)).astype(F32) for v in pcol]
    chip_row = two * chip

    def row_inside(start):
        r = chip_row + start + sub
        return ((r >= 0) & (r < rows * tiles)).astype(F32)

    def halo_up(x, i, l):
        return rdma(
            x.at[l, :, pl.ds(24, REACH)], x.at[l, :, pl.ds(24 + two, REACH)],
            hsend.at[i, l, 0], hrecv.at[i, l, 0], (lay, prev0 + h),
        )

    def halo_down(x, i, l):
        return rdma(
            x.at[l, :, pl.ds(24 + two - REACH, REACH)], x.at[l, :, pl.ds(24 - REACH, REACH)],
            hsend.at[i, l, 1], hrecv.at[i, l, 1], (lay, next0 + h),
        )

    def send_halo(x, i, l):
        @pl.when(has_prev)
        def _():
            halo_up(x, i, l).start()

        @pl.when(has_next)
        def _():
            halo_down(x, i, l).start()

    def wait_halo(x, i, l):
        @pl.when(has_prev)
        def _():
            halo_down(x, i, l).wait_recv()

        @pl.when(has_next)
        def _():
            halo_up(x, i, l).wait_recv()

    def piece(i, l, half):
        src = ya.at[i, l, pl.ds(at * rows * half, at * rows)].reshape(rows, at, 128)
        dst = outs[i].at[:, pl.ds(at * (2 * lay + h), at)]
        return src, dst

    def send_pieces(i, l):
        for half in range(2):
            src, dst = piece(i, l, half)
            here = (l == lay) & (half == h)

            @pl.when(here)
            def _():
                pltpu.make_async_copy(src, dst, tlocal.at[i]).start()

            @pl.when(jnp.logical_not(here))
            def _():
                rdma(src, dst, tsend.at[i], trecv.at[i], (l, 2 * chip + half)).start()

    def stage(i, l, rb, value):
        turned = [pltpu.roll(v, MARGIN, 1) for v in value]
        for k in range(at):
            ya[i, l, pl.ds(at * 8 * rb + k, 8, stride=at), :] = jnp.where(lane < MARGIN, turned[k], turned[k + 1])

    def finish_b(l, acc):
        part_sib(l).wait_recv()

        @pl.when(has_prev)
        def _():
            part_down(l, 0).wait_recv()

        @pl.when(has_next)
        def _():
            part_up(l, 0).wait_recv()

        for rb in range(two // 8):
            value = []
            for j in range(nt):
                v = cb[h, l, j, pl.ds(16 + 8 * rb - rows * h, 8), :]
                v = v + sib[l, j, pl.ds(16 + 8 * rb - rows * (1 - h), 8), :]
                if rb < 2:
                    v = v + prv[l, j, 8 * rb : 8 * rb + 8, :]
                if rb == two // 8 - 1:
                    v = v + nxt[l, j]
                v = v * x_in[j]
                acc = acc + x_own[j] * (v * v)
                x0[l, j, 24 + 8 * rb : 32 + 8 * rb, :] = v
                value.append(v)
            stage(0, l, rb, value)
        send_halo(x0, 0, l)
        return acc

    bb = lax.fori_loop(0, lays, finish_b, zero)

    mask_sib().wait_recv()

    @pl.when(has_prev)
    def _():
        mask_down(0).wait_recv()

    @pl.when(has_next)
    def _():
        mask_up(0).wait_recv()

    def beside(value):
        n = len(value)
        r = [pltpu.roll(v, 1, 1) for v in value]
        l = [pltpu.roll(v, 127, 1) for v in value]
        left = [jnp.where(lane >= 1, r[j], r[(j - 1) % n]) for j in range(n)]
        right = [jnp.where(lane < 127, l[j], l[(j + 1) % n]) for j in range(n)]
        return left, right

    def front(x, i):
        def smooth(l, acc):
            wait_halo(x, i, l)
            part = zero
            for rb in range(4):
                row = -1 + 8 * rb
                mid = [x[l, j, 24 + row : 32 + row, :] for j in range(nt)]
                left, right = beside(mid)
                inside = row_inside(row)
                own = ((row + sub >= 0) & (row + sub < two)).astype(F32)
                for j in range(nt):
                    v = 4.0 * mid[j] - x[l, j, 23 + row : 31 + row, :] - x[l, j, 25 + row : 33 + row, :]
                    v = (v - left[j] - right[j]) * (inside * x_in[j])
                    lb[l, j, 8 * rb : 8 * rb + 8, :] = v
                    part = part + (own * x_own[j]) * (v * v)
            return acc + reg[l] * part

        energy = lax.fori_loop(0, lays, smooth, zero)

        def give(l, c):
            send_pieces(i, l)
            return c

        lax.fori_loop(0, lays, give, 0)

        def project(g, acc):
            for rb in range(6):
                total = [zero] * nt
                for l in range(lays):
                    a, s = off[l, 0, g], HALO - off[l, 1, g]
                    start = 15 + 8 * rb + a
                    turned = [pltpu.roll(x[l, j, pl.ds(start, 8), :], s, 1) for j in range(nt)]
                    keep = lane >= s
                    total = [total[j] + jnp.where(keep, turned[j], turned[(j - 1) % nt]) for j in range(nt)]
                inside = row_inside(8 * rb - 9)
                total = [total[j] * (inside * p_in[j]) for j in range(nt)]
                turned = [pltpu.roll(v, 127, 1) for v in total]
                for j in range(nt):
                    pb[0, j, 8 * rb : 8 * rb + 8, :] = total[j]
                    pb[1, j, 8 * rb : 8 * rb + 8, :] = jnp.where(lane < 127, turned[j], turned[(j + 1) % nt])
            for rb in range(5):
                up, lo, dn = 8 * rb, 8 * rb + 1, 8 * rb + 2
                turned, rest = [], []
                inside = row_inside(8 * rb - 8)
                for j in range(nt):
                    m_lo, m_up = mb[j, lo : lo + 8, :], mb[j, up : up + 8, :]
                    p_lo, r_lo = pb[0, j, lo : lo + 8, :], pb[1, j, lo : lo + 8, :]
                    e1 = m_lo * (pb[1, j, dn : dn + 8, :] - p_lo)
                    e2 = m_lo * (r_lo - pb[0, j, dn : dn + 8, :])
                    e1_up = m_up * (r_lo - pb[0, j, up : up + 8, :])
                    e2_up = m_up * (pb[1, j, up : up + 8, :] - p_lo)
                    if 1 <= rb <= two // 8:
                        acc = acc + (0.5 * p_own[j]) * (e1 * e1 + e2 * e2)
                    turned.append(pltpu.roll(e1_up + e2, 1, 1))
                    rest.append(e1 + e2_up)
                for j in range(nt):
                    f = jnp.where(lane >= 1, turned[j], turned[(j - 1) % nt])
                    qb[g, j, 8 * rb : 8 * rb + 8, :] = (f - rest[j]) * (0.5 * inside * p_in[j])
            return acc

        return lax.fori_loop(0, dirs, project, energy)

    def back(i, x_next, first, last, acc):
        def layer(l, acc):
            for rb in range(two // 8):
                total = [zero] * nt
                for g in range(dirs):
                    a, s = off[l, 0, g], lax.rem(120 + off[l, 1, g], 128)
                    start = 8 + 8 * rb - a
                    turned = [pltpu.roll(qb[g, j, pl.ds(start, 8), :], s, 1) for j in range(nt)]
                    keep = lane < 120 + off[l, 1, g]
                    total = [total[j] + jnp.where(keep, turned[j], turned[(j + 1) % nt]) for j in range(nt)]
                lo = 8 * rb + 1
                mid = [lb[l, j, lo : lo + 8, :] for j in range(nt)]
                left, right = beside(mid)
                value = []
                for j in range(nt):
                    v = 4.0 * mid[j] - lb[l, j, lo - 1 : lo + 7, :] - lb[l, j, lo + 1 : lo + 9, :] - left[j] - right[j]
                    v = (total[j] + reg[l] * v) * x_in[j]
                    if x_next is not None:
                        acc = acc + x_own[j] * (v * v)
                        x_next[l, j, 24 + 8 * rb : 32 + 8 * rb, :] = v
                    value.append(v)
                stage(i, l, rb, value)
            if x_next is not None:
                send_halo(x_next, 1, l)
            else:
                send_pieces(i, l)
            return acc

        return lax.fori_loop(first, last, layer, acc)

    e0 = front(x0, 0)
    yy = back(1, x1, 0, lays, zero)
    e1 = front(x1, 1)

    lane1 = lane[0:1]

    def whole(v):
        return jnp.sum(jnp.sum(v, axis=0, keepdims=True), axis=1, keepdims=True)

    packed = jnp.zeros((1, 128), F32)
    for k, v in enumerate((bb, e0, yy, e1)):
        packed = jnp.where(lane1 == k, whole(v), packed)
    arsrc[0:1, :] = packed

    def exchange(stage_id, slots, count, member):
        def one(d, c):
            rdma(
                arsrc.at[pl.ds(8 * stage_id, 1)], slots.at[pl.ds(count - 1 - d, 1)],
                asend.at[stage_id], arecv.at[stage_id], member(d),
            ).start()
            return c

        lax.fori_loop(1, count, one, 0)

    exchange(0, ar1, g1, member1)
    back(2, None, 0, lays, zero)
    wait_bytes(ar1, arecv.at[0])
    arsrc[8:9, :] = arsrc[0:1, :] + jnp.sum(ar1[...], axis=0, keepdims=True)
    exchange(1, ar2, g2, member2)
    wait_bytes(ar2, arecv.at[1])
    total = arsrc[8:9, :] + jnp.sum(ar2[...], axis=0, keepdims=True)
    bb, e0, yy, e1 = (jnp.sum(jnp.where(lane1 == k, total, 0.0), axis=1, keepdims=True) for k in range(4))
    a0 = bb / e0
    rr = a0 * a0 * yy - bb
    beta = rr / bb
    grown = 1.0 + beta
    a1 = rr / (grown * grown * e0 - 2.0 * a0 * grown * yy + a0 * a0 * e1)
    k0_ref[...] = jnp.broadcast_to(a0 + a1 * grown, (1, 128))
    k1_ref[...] = jnp.broadcast_to(a0 * a1, (1, 128))

    for i in range(3):
        wait_bytes(outs[i].at[:, pl.ds(0, at * (2 * nl - 1))], trecv.at[i])
        src, dst = piece(i, 0, 0)
        pltpu.make_async_copy(src, dst, tlocal.at[i]).wait()

    mask_sib().wait_send()

    @pl.when(sends_down)
    def _():
        mask_down(0).wait_send()
        mask_down(1).wait_send()

    @pl.when(sends_up)
    def _():
        mask_up(0).wait_send()
        mask_up(1).wait_send()

    def drain(l, c):
        part_sib(l).wait_send()

        @pl.when(sends_down)
        def _():
            part_down(l, 0).wait_send()
            part_down(l, 1).wait_send()

        @pl.when(sends_up)
        def _():
            part_up(l, 0).wait_send()
            part_up(l, 1).wait_send()

        for i, x in enumerate((x0, x1)):

            @pl.when(has_prev)
            def _():
                halo_up(x, i, l).wait_send()

            @pl.when(has_next)
            def _():
                halo_down(x, i, l).wait_send()

        return c

    lax.fori_loop(0, lays, drain, 0)
    for i in range(3):
        wait_bytes(outs[i].at[:, pl.ds(0, at * (2 * nl - 1))], tsend.at[i])
    wait_bytes(ar1, asend.at[0])
    wait_bytes(ar2, asend.at[1])


def per_device(shape, measured_slopes, valid_mask, layer_offsets, reg_weight):
    nl, tiles = shape
    dirs, _, rows, cols = measured_slopes.shape
    lays = layer_offsets.shape[1]
    width = cols // (2 * nl)
    at = width // 128
    nt, st = at + 1, 2 * at + 2
    zs = 2 if tiles % 16 == 0 else 1
    g1, g2 = nl * zs * 2, tiles // (zs * 2)
    vm = lambda *s: pltpu.VMEM(s, F32)
    dma = lambda *s: pltpu.SemaphoreType.DMA(s)
    out = jax.ShapeDtypeStruct((rows, cols // 128, 128), F32)
    slopes = measured_slopes.reshape(dirs, 2, rows, cols // 128, 128).transpose(0, 2, 3, 1, 4)
    slopes = slopes.reshape(dirs, rows, cols // 64, 128)
    b, y1, y2, k0, k1 = pl.pallas_call(
        functools.partial(kernel, (dirs, lays, tiles, rows, cols, nl)),
        out_shape=(out,) * 3 + (jax.ShapeDtypeStruct((1, 128), F32),) * 2,
        in_specs=[pl.BlockSpec(memory_space=pltpu.HBM)] * 2 + [pl.BlockSpec(memory_space=pltpu.SMEM)] * 2,
        out_specs=(pl.BlockSpec(memory_space=pltpu.HBM),) * 3 + (pl.BlockSpec(memory_space=pltpu.VMEM),) * 2,
        scratch_shapes=[
            vm(dirs, 2 * st, rows + 4, 128),
            pltpu.VMEM((rows, 128 * st), jnp.int32),
            vm(2, st, 32, 128),
            vm(dirs, st, 48, 128),
            vm(2, lays, nt, 40, 128),
            vm(lays, nt, 40, 128),
            vm(lays, nt, 16, 128),
            vm(lays, nt, 8, 128),
            vm(2, nt, 16, 128),
            vm(nt, 56, 128),
            vm(lays, nt, 72, 128),
            vm(lays, nt, 72, 128),
            vm(2, nt, 48, 128),
            vm(dirs, nt, 40, 128),
            vm(lays, nt, 32, 128),
            vm(3, lays, at * 2 * rows, 128),
            vm(16, 128),
            vm(g1 - 1, 128),
            vm(g2 - 1, 128),
            dma(2), dma(3), dma(3), dma(lays, 3), dma(lays, 3), dma(2, lays, 2), dma(2, lays, 2),
            dma(3), dma(3), dma(3), dma(2), dma(2),
        ],
        compiler_params=pltpu.CompilerParams(
            collective_id=0, has_side_effects=True, vmem_limit_bytes=56 * 1024 * 1024
        ),
    )(slopes, valid_mask, layer_offsets.transpose(1, 2, 0), reg_weight)
    est = k0 * b - k1 * y1
    res = b - k0 * y1 + k1 * y2
    return est.reshape(1, rows, cols), res.reshape(1, rows, cols)


def solution(mesh):
    return jax.shard_map(
        functools.partial(per_device, (mesh.shape["layer"], mesh.shape["tile"])),
        mesh=mesh,
        in_specs=(P(None, None, "tile", None), P("tile", None), P(), P()),
        out_specs=(P("layer", "tile", None), P("layer", "tile", None)),
        check_vma=False,
    )
```

```python
import functools

import jax
import jax.numpy as jnp
from jax import lax
from jax.experimental import pallas as pl
from jax.experimental.pallas import tpu as pltpu
from jax.sharding import PartitionSpec as P

MESH = pl.DeviceIdType.MESH
F32 = jnp.float32
HALO = 8
MARGIN = 64
ITERS = 2
REACH = 17


def kernel(
    cfg,
    slopes_hbm, mask_hbm, off, reg,
    fields, k0_ref, k1_ref,
    sl, mki, eb, q0, cb, sib, prv, nxt, ms, mb, xb, xw, sums, pb, qb, lb, ya, arsrc, ar1, ar2,
    in_sem, msend, mrecv, csend, crecv, hsend, hrecv, tsend, trecv, tlocal, asend, arecv,
):
    dirs, lays, tiles, rows, cols, nl = cfg
    two = 2 * rows
    width = cols // (2 * nl)
    at = width // 128
    nt = at + 1
    st = 2 * at + 2
    zs, xs = (2, 4) if tiles % 16 == 0 else (1, tiles // 2)
    g1 = nl * zs * 2
    g2 = tiles // (zs * 2)
    lay = lax.axis_index("layer")
    t = lax.axis_index("tile")
    chip = lax.div(t, 2)
    h = lax.rem(t, 2)
    chips = tiles // 2
    has_prev = chip > 0
    has_next = chip < chips - 1
    prev0 = 2 * chip - 2
    next0 = 2 * chip + 2
    lane = lax.broadcasted_iota(jnp.int32, (8, 128), 1)
    sub = lax.broadcasted_iota(jnp.int32, (8, 128), 0)
    zero = jnp.zeros((8, 128), F32)

    def rdma(src, dst, ss, rs, dev):
        return pltpu.make_async_remote_copy(
            src_ref=src, dst_ref=dst, send_sem=ss, recv_sem=rs, device_id=dev, device_id_type=MESH
        )

    def wait_bytes(ref, sem):
        pltpu.make_async_copy(ref, ref, sem).wait()

    barrier = pltpu.get_barrier_semaphore()

    def greet(dev):
        pl.semaphore_signal(barrier, inc=1, device_id=dev, device_id_type=MESH)

    other = 2 * chip + 1 - h

    @pl.when(has_prev)
    def _():
        greet((lay, prev0))
        greet((lay, prev0 + 1))

    @pl.when(has_next)
    def _():
        greet((lay, next0))
        greet((lay, next0 + 1))

    tx, tz, ty = lax.rem(chip, xs), lax.rem(lax.div(chip, xs), zs), lax.div(chip, xs * zs)
    me1 = (lay * zs + tz) * 2 + h
    me2 = ty * xs + tx

    def tile_at(y, z, x, core):
        return ((y * zs + z) * xs + x) * 2 + core

    def member1(d):
        index = lax.rem(me1 + d, g1)
        there = lax.div(index, 2 * zs)
        return (there, tile_at(ty, lax.rem(lax.div(index, 2), zs), tx, lax.rem(index, 2)))

    def member2(d):
        index = lax.rem(me2 + d, g2)
        return (lay, tile_at(lax.div(index, xs), tz, lax.rem(index, xs), h))

    def greet1(d, c):
        greet(member1(d))
        return c

    def greet2(d, c):
        greet(member2(d))
        return c

    lax.fori_loop(1, g1, greet1, 0)
    lax.fori_loop(1, g2, greet2, 0)

    span = 2 * width

    def mask_in(first, count, at_tile):
        src, dst = pl.ds(pl.multiple_of(first, 128), count), pl.ds(128 * at_tile, count)
        return pltpu.make_async_copy(mask_hbm.at[:, src], mki.at[:, dst], in_sem.at[0])

    def slopes_in(first, count, at_tile):
        src, dst = pl.ds(lax.div(first, 64), count // 64), pl.ds(2 * at_tile, count // 64)

        def one(i, c):
            pltpu.make_async_copy(slopes_hbm.at[:, i, src], sl.at[:, dst, i], in_sem.at[1]).start()
            return c

        lax.fori_loop(0, rows, one, 0)

    def slopes_wait(first, count, at_tile):
        dst = sl.at[:, pl.ds(2 * at_tile, count // 64), pl.ds(0, rows)]
        pltpu.make_async_copy(dst, dst, in_sem.at[1]).wait()

    def cases(act):
        @pl.when(lay == 0)
        def _():
            act(0, span + 128, 1)

        @pl.when(lay == nl - 1)
        def _():
            act(span * (nl - 1) - 128, span + 128, 0)

        @pl.when((lay > 0) & (lay < nl - 1))
        def _():
            act(span * lay - 128, span + 256, 0)

    cases(lambda *w: mask_in(*w).start())
    cases(slopes_in)

    @pl.when(lay == 0)
    def _():
        mki[:, 0:128] = jnp.zeros((rows, 128), jnp.int32)
        sl[:, 0:2, 0:rows] = jnp.zeros((dirs, 2, rows, 128), F32)

    @pl.when(lay == nl - 1)
    def _():
        mki[:, 128 * (st - 1) :] = jnp.zeros((rows, 128), jnp.int32)
        sl[:, 2 * st - 2 :, 0:rows] = jnp.zeros((dirs, 2, rows, 128), F32)

    sib[:, :, 0:8] = jnp.zeros((lays, nt, 8, 128), F32)
    sib[:, :, rows + 25 : 40] = jnp.zeros((lays, nt, 15 - rows, 128), F32)
    prv[:, :, HALO + 1 : 16] = jnp.zeros((lays, nt, 15 - HALO, 128), F32)
    mb[:, HALO + 1 + two + HALO :] = jnp.zeros((nt, 56 - two - 2 * HALO - 1, 128), F32)

    @pl.when(jnp.logical_not(has_prev))
    def _():
        prv[:, :, 0 : HALO + 1] = jnp.zeros((lays, nt, HALO + 1, 128), F32)
        mb[:, 0 : HALO + 1] = jnp.zeros((nt, HALO + 1, 128), F32)
        xb[0:2, :, :, 0:24] = jnp.zeros((2, lays, nt, 24, 128), F32)

    @pl.when(jnp.logical_not(has_next))
    def _():
        nxt[...] = jnp.zeros_like(nxt)
        mb[:, HALO + 1 + two : HALO + 1 + two + HALO] = jnp.zeros((nt, HALO, 128), F32)
        xb[0:2, :, :, 24 + two :] = jnp.zeros((2, lays, nt, 48 - two, 128), F32)

    eb[:, :, 0:8] = jnp.zeros((2, st, 8, 128), F32)
    eb[:, :, 16:24] = jnp.zeros((2, st, 8, 128), F32)
    q0[:, :, 0:16] = jnp.zeros((dirs, st, 16, 128), F32)
    q0[:, :, 32:48] = jnp.zeros((dirs, st, 16, 128), F32)
    cb[:, :, :, 0:8, :] = jnp.zeros((2, lays, nt, 8, 128), F32)

    cases(lambda *w: mask_in(*w).wait())
    bands = [slice(0, 8), slice(8, rows)]
    for k in range(2):
        for band in bands:
            turned = [
                pltpu.roll(mki[band, 128 * j : 128 * j + 128].astype(F32), MARGIN + HALO, 1)
                for j in range(at * k, at * k + nt + 1)
            ]
            keep = lane[: band.stop - band.start] < MARGIN + HALO
            for j in range(nt):
                ms[k, j, band, :] = jnp.where(keep, turned[j], turned[j + 1])
    mine = HALO + 1 + rows * h
    for j in range(nt):
        mb[j, pl.ds(mine, rows), :] = ms[h, j, 0:rows, :]
    def mask_sib():
        return rdma(
            ms.at[1 - h, :, pl.ds(0, rows)], mb.at[:, pl.ds(mine, rows)], msend.at[0], mrecv.at[0], (lay, other)
        )

    def mask_down(k):
        return rdma(
            ms.at[k, :, pl.ds(rows - HALO - 1, HALO + 1)], mb.at[:, pl.ds(0, HALO + 1)],
            msend.at[1 + k], mrecv.at[1], (lay, next0 + k),
        )

    def mask_up(k):
        return rdma(
            ms.at[k, :, pl.ds(0, HALO)], mb.at[:, pl.ds(HALO + 1 + two, HALO)],
            msend.at[1 + k], mrecv.at[2], (lay, prev0 + k),
        )

    sends_down = has_next & (h == 1)
    sends_up = has_prev & (h == 0)
    cases(slopes_wait)
    first_row = rows * t

    def own_adjoint(g, c):
        for band in bands:
            for j in range(st):
                at_cols = slice(128 * j, 128 * j + 128)
                m = mki[band, at_cols].astype(F32)
                u = m * sl[g, 2 * j, band, :]
                w = m * sl[g, 2 * j + 1, band, :]
                eb[0, j, 8 + band.start : 8 + band.stop, :] = u + w
                eb[1, j, 8 + band.start : 8 + band.stop, :] = u - w
        for rb in range(2):
            lo, up = 8 + 8 * rb, 7 + 8 * rb
            row_in = (first_row + 8 * rb + sub < rows * tiles).astype(F32)
            right = []
            for j in range(st):
                right.append(pltpu.roll(eb[0, j, up : up + 8, :] + eb[1, j, lo : lo + 8, :], 1, 1))
            for j in range(st):
                f = jnp.where(lane >= 1, right[j], right[max(j - 1, 0)])
                q = 0.5 * (f - eb[0, j, lo : lo + 8, :] - eb[1, j, up : up + 8, :])
                col_in = (span * lay - 128 + 128 * j + lane < cols).astype(F32)
                q0[g, j, 16 + 8 * rb : 24 + 8 * rb, :] = q * (row_in * col_in)
        return c

    lax.fori_loop(0, dirs, own_adjoint, 0)
    pl.semaphore_wait(
        barrier,
        2 * has_prev.astype(jnp.int32) + 2 * has_next.astype(jnp.int32) + (g1 - 1) + (g2 - 1),
    )

    mask_sib().start()

    @pl.when(sends_down)
    def _():
        mask_down(0).start()
        mask_down(1).start()

    @pl.when(sends_up)
    def _():
        mask_up(0).start()
        mask_up(1).start()


    def part_sib(l):
        return rdma(
            cb.at[1 - h, l, :, pl.ds(8, rows + 17)], sib.at[l, :, pl.ds(8, rows + 17)],
            csend.at[l, 0], crecv.at[l, 0], (lay, other),
        )

    def part_down(l, k):
        return rdma(
            cb.at[k, l, :, pl.ds(16 + rows, 9)], prv.at[l, :, pl.ds(0, 9)],
            csend.at[l, 1 + k], crecv.at[l, 1], (lay, next0 + k),
        )

    def part_up(l, k):
        return rdma(
            cb.at[k, l, :, pl.ds(8, 8)], nxt.at[l], csend.at[l, 1 + k], crecv.at[l, 2], (lay, prev0 + k)
        )

    def blocks(l, first):
        for k8 in range(2):
            at8 = pl.multiple_of(8 * (first + k8), 8)
            total = [[zero] * nt, [zero] * nt]
            for g in range(dirs):
                a, s = off[l, 0, g], MARGIN + off[l, 1, g]
                start = 8 + at8 - a
                turned = [pltpu.roll(q0[g, j, pl.ds(start, 8), :], s, 1) for j in range(st)]
                keep = lane < s
                for k in range(2):
                    for j in range(nt):
                        total[k][j] = total[k][j] + jnp.where(keep, turned[at * k + j], turned[at * k + j + 1])
            for k in range(2):
                for j in range(nt):
                    cb[k, l, j, pl.ds(8 + at8, 8), :] = total[k][j]

    def parts(step, c):
        l, last = lax.rem(step, lays), lax.div(step, lays)
        blocks(l, 2 * lax.rem(h + last, 2))

        @pl.when((last == 0) & sends_down)
        def _():
            part_down(l, 0).start()
            part_down(l, 1).start()

        @pl.when((last == 0) & sends_up)
        def _():
            part_up(l, 0).start()
            part_up(l, 1).start()

        @pl.when(last == 1)
        def _():
            part_sib(l).start()

        return c

    lax.fori_loop(0, 2 * lays, parts, 0)

    c0 = width * (2 * lay + h)
    xcol = [c0 - MARGIN + 128 * j + lane for j in range(nt)]
    x_in = [((v >= 0) & (v < cols)).astype(F32) for v in xcol]
    x_own = [((v >= c0) & (v < c0 + width)).astype(F32) for v in xcol]
    pcol = [c0 - MARGIN - HALO + 128 * j + lane for j in range(nt)]
    p_in = [((v >= 0) & (v < cols)).astype(F32) for v in pcol]
    p_own = [((v >= c0) & (v < c0 + width)).astype(F32) for v in pcol]
    chip_row = two * chip

    def row_inside(start):
        r = chip_row + start + sub
        return ((r >= 0) & (r < rows * tiles)).astype(F32)

    def halo_up(i, l):
        return rdma(
            xb.at[i, l, :, pl.ds(24, REACH)], xb.at[i, l, :, pl.ds(24 + two, REACH)],
            hsend.at[i, l, 0], hrecv.at[i, l, 0], (lay, prev0 + h),
        )

    def halo_down(i, l):
        return rdma(
            xb.at[i, l, :, pl.ds(24 + two - REACH, REACH)], xb.at[i, l, :, pl.ds(24 - REACH, REACH)],
            hsend.at[i, l, 1], hrecv.at[i, l, 1], (lay, next0 + h),
        )

    def send_halo(i, l):
        @pl.when(has_prev)
        def _():
            halo_up(i, l).start()

        @pl.when(has_next)
        def _():
            halo_down(i, l).start()

    def wait_halo(i, l):
        @pl.when(has_prev)
        def _():
            halo_down(i, l).wait_recv()

        @pl.when(has_next)
        def _():
            halo_up(i, l).wait_recv()

    def piece(i, l, half):
        src = ya.at[i, l, pl.ds(at * rows * half, at * rows)].reshape(rows, at, 128)
        dst = fields.at[i, :, pl.ds(at * (2 * lay + h), at)]
        return src, dst

    def send_pieces(i, l):
        for half in range(2):
            src, dst = piece(i, l, half)
            here = (l == lay) & (half == h)

            @pl.when(here)
            def _():
                pltpu.make_async_copy(src, dst, tlocal.at[i]).start()

            @pl.when(jnp.logical_not(here))
            def _():
                rdma(src, dst, tsend.at[i], trecv.at[i], (l, 2 * chip + half)).start()

    def stage(i, l, rb, value):
        turned = [pltpu.roll(v, MARGIN, 1) for v in value]
        for k in range(at):
            ya[i, l, pl.ds(at * 8 * rb + k, 8, stride=at), :] = jnp.where(lane < MARGIN, turned[k], turned[k + 1])

    def finish_b(l, acc):
        part_sib(l).wait_recv()

        @pl.when(has_prev)
        def _():
            part_down(l, 0).wait_recv()

        @pl.when(has_next)
        def _():
            part_up(l, 0).wait_recv()

        for rb in range(two // 8):
            value = []
            for j in range(nt):
                v = cb[h, l, j, pl.ds(16 + 8 * rb - rows * h, 8), :]
                v = v + sib[l, j, pl.ds(16 + 8 * rb - rows * (1 - h), 8), :]
                if rb < 2:
                    v = v + prv[l, j, 8 * rb : 8 * rb + 8, :]
                if rb == two // 8 - 1:
                    v = v + nxt[l, j]
                v = v * x_in[j]
                acc = acc + x_own[j] * (v * v)
                xb[0, l, j, 24 + 8 * rb : 32 + 8 * rb, :] = v
                value.append(v)
            stage(0, l, rb, value)
        send_halo(0, l)
        return acc

    sums[0] = lax.fori_loop(0, lays, finish_b, zero)

    mask_sib().wait_recv()

    @pl.when(has_prev)
    def _():
        mask_down(0).wait_recv()

    @pl.when(has_next)
    def _():
        mask_up(0).wait_recv()

    def beside(value):
        n = len(value)
        r = [pltpu.roll(v, 1, 1) for v in value]
        l = [pltpu.roll(v, 127, 1) for v in value]
        left = [jnp.where(lane >= 1, r[j], r[(j - 1) % n]) for j in range(n)]
        right = [jnp.where(lane < 127, l[j], l[(j + 1) % n]) for j in range(n)]
        return left, right

    def front(i):
        def smooth(l, acc):
            wait_halo(i, l)
            for j in range(nt):
                xw[l, j] = xb[i, l, j]
            part = zero
            for rb in range(4):
                row = -1 + 8 * rb
                mid = [xb[i, l, j, 24 + row : 32 + row, :] for j in range(nt)]
                left, right = beside(mid)
                inside = row_inside(row)
                own = ((row + sub >= 0) & (row + sub < two)).astype(F32)
                for j in range(nt):
                    v = 4.0 * mid[j] - xb[i, l, j, 23 + row : 31 + row, :] - xb[i, l, j, 25 + row : 33 + row, :]
                    v = (v - left[j] - right[j]) * (inside * x_in[j])
                    lb[l, j, 8 * rb : 8 * rb + 8, :] = v
                    part = part + (own * x_own[j]) * (v * v)
            return acc + reg[l] * part

        energy = lax.fori_loop(0, lays, smooth, zero)

        def give(l, c):
            send_pieces(i, l)
            return c

        lax.fori_loop(0, lays, give, 0)

        def project(g, acc):
            for rb in range(6):
                total = [zero] * nt
                for l in range(lays):
                    a, s = off[l, 0, g], HALO - off[l, 1, g]
                    start = 15 + 8 * rb + a
                    turned = [pltpu.roll(xw[l, j, pl.ds(start, 8), :], s, 1) for j in range(nt)]
                    keep = lane >= s
                    total = [total[j] + jnp.where(keep, turned[j], turned[(j - 1) % nt]) for j in range(nt)]
                inside = row_inside(8 * rb - 9)
                total = [total[j] * (inside * p_in[j]) for j in range(nt)]
                turned = [pltpu.roll(v, 127, 1) for v in total]
                for j in range(nt):
                    pb[0, j, 8 * rb : 8 * rb + 8, :] = total[j]
                    pb[1, j, 8 * rb : 8 * rb + 8, :] = jnp.where(lane < 127, turned[j], turned[(j + 1) % nt])
            for rb in range(5):
                up, lo, dn = 8 * rb, 8 * rb + 1, 8 * rb + 2
                turned, rest = [], []
                inside = row_inside(8 * rb - 8)
                for j in range(nt):
                    m_lo, m_up = mb[j, lo : lo + 8, :], mb[j, up : up + 8, :]
                    p_lo, r_lo = pb[0, j, lo : lo + 8, :], pb[1, j, lo : lo + 8, :]
                    e1 = m_lo * (pb[1, j, dn : dn + 8, :] - p_lo)
                    e2 = m_lo * (r_lo - pb[0, j, dn : dn + 8, :])
                    e1_up = m_up * (r_lo - pb[0, j, up : up + 8, :])
                    e2_up = m_up * (pb[1, j, up : up + 8, :] - p_lo)
                    if 1 <= rb <= two // 8:
                        acc = acc + (0.5 * p_own[j]) * (e1 * e1 + e2 * e2)
                    turned.append(pltpu.roll(e1_up + e2, 1, 1))
                    rest.append(e1 + e2_up)
                for j in range(nt):
                    f = jnp.where(lane >= 1, turned[j], turned[(j - 1) % nt])
                    qb[g, j, 8 * rb : 8 * rb + 8, :] = (f - rest[j]) * (0.5 * inside * p_in[j])
            return acc

        return lax.fori_loop(0, dirs, project, energy)

    def back(i):
        def layer(l, acc):
            for rb in range(two // 8):
                total = [zero] * nt
                for g in range(dirs):
                    a, s = off[l, 0, g], lax.rem(120 + off[l, 1, g], 128)
                    start = 8 + 8 * rb - a
                    turned = [pltpu.roll(qb[g, j, pl.ds(start, 8), :], s, 1) for j in range(nt)]
                    keep = lane < 120 + off[l, 1, g]
                    total = [total[j] + jnp.where(keep, turned[j], turned[(j + 1) % nt]) for j in range(nt)]
                lo = 8 * rb + 1
                mid = [lb[l, j, lo : lo + 8, :] for j in range(nt)]
                left, right = beside(mid)
                value = []
                for j in range(nt):
                    v = 4.0 * mid[j] - lb[l, j, lo - 1 : lo + 7, :] - lb[l, j, lo + 1 : lo + 9, :] - left[j] - right[j]
                    v = (total[j] + reg[l] * v) * x_in[j]
                    acc = acc + x_own[j] * (v * v)
                    xb[i, l, j, 24 + 8 * rb : 32 + 8 * rb, :] = v
                    value.append(v)
                stage(i, l, rb, value)

            @pl.when(i < ITERS)
            def _():
                send_halo(i, l)

            @pl.when(i == ITERS)
            def _():
                send_pieces(i, l)

            return acc

        return lax.fori_loop(0, lays, layer, zero)

    lane1 = lane[0:1]

    def whole(v):
        return jnp.sum(jnp.sum(v, axis=0, keepdims=True), axis=1, keepdims=True)

    def exchange(stage_id, slots, count, member):
        def one(d, c):
            rdma(
                arsrc.at[pl.ds(8 * stage_id, 1)], slots.at[pl.ds(count - 1 - d, 1)],
                asend.at[stage_id], arecv.at[stage_id], member(d),
            ).start()
            return c

        lax.fori_loop(1, count, one, 0)

    def apply(i, c):
        sums[1 + i] = front(i)

        @pl.when(i == ITERS - 1)
        def _():
            packed = jnp.zeros((1, 128), F32)
            for k, n in enumerate((0, 1, 3, 2)):
                packed = jnp.where(lane1 == k, whole(sums[n]), packed)
            arsrc[0:1, :] = packed
            exchange(0, ar1, g1, member1)

        sums[3 + i] = back(i + 1)
        return c

    lax.fori_loop(0, ITERS, apply, 0)
    wait_bytes(ar1, arecv.at[0])
    arsrc[8:9, :] = arsrc[0:1, :] + jnp.sum(ar1[...], axis=0, keepdims=True)
    exchange(1, ar2, g2, member2)
    wait_bytes(ar2, arecv.at[1])
    total = arsrc[8:9, :] + jnp.sum(ar2[...], axis=0, keepdims=True)
    bb, e0, yy, e1 = (jnp.sum(jnp.where(lane1 == k, total, 0.0), axis=1, keepdims=True) for k in range(4))
    a0 = bb / e0
    rr = a0 * a0 * yy - bb
    beta = rr / bb
    grown = 1.0 + beta
    a1 = rr / (grown * grown * e0 - 2.0 * a0 * grown * yy + a0 * a0 * e1)
    k0_ref[...] = jnp.broadcast_to(a0 + a1 * grown, (1, 128))
    k1_ref[...] = jnp.broadcast_to(a0 * a1, (1, 128))

    for i in range(3):
        wait_bytes(fields.at[i, :, pl.ds(0, at * (2 * nl - 1))], trecv.at[i])
        src, dst = piece(i, 0, 0)
        pltpu.make_async_copy(src, dst, tlocal.at[i]).wait()

    mask_sib().wait_send()

    @pl.when(sends_down)
    def _():
        mask_down(0).wait_send()
        mask_down(1).wait_send()

    @pl.when(sends_up)
    def _():
        mask_up(0).wait_send()
        mask_up(1).wait_send()

    def drain(l, c):
        part_sib(l).wait_send()

        @pl.when(sends_down)
        def _():
            part_down(l, 0).wait_send()
            part_down(l, 1).wait_send()

        @pl.when(sends_up)
        def _():
            part_up(l, 0).wait_send()
            part_up(l, 1).wait_send()

        for i in range(ITERS):

            @pl.when(has_prev)
            def _():
                halo_up(i, l).wait_send()

            @pl.when(has_next)
            def _():
                halo_down(i, l).wait_send()

        return c

    lax.fori_loop(0, lays, drain, 0)
    for i in range(3):
        wait_bytes(fields.at[i, :, pl.ds(0, at * (2 * nl - 1))], tsend.at[i])
    wait_bytes(ar1, asend.at[0])
    wait_bytes(ar2, asend.at[1])


def combine(fields, k0, k1, est, res):
    a, c = k0[...], k1[...]
    for r in range(fields.shape[1]):
        b, y1, y2 = fields[0, r], fields[1, r], fields[2, r]
        est[r] = a * b - c * y1
        res[r] = b - a * y1 + c * y2


def per_device(shape, measured_slopes, valid_mask, layer_offsets, reg_weight):
    nl, tiles = shape
    dirs, _, rows, cols = measured_slopes.shape
    lays = layer_offsets.shape[1]
    width = cols // (2 * nl)
    at = width // 128
    nt, st = at + 1, 2 * at + 2
    zs = 2 if tiles % 16 == 0 else 1
    g1, g2 = nl * zs * 2, tiles // (zs * 2)
    vm = lambda *s: pltpu.VMEM(s, F32)
    dma = lambda *s: pltpu.SemaphoreType.DMA(s)
    out = jax.ShapeDtypeStruct((3, rows, cols // 128, 128), F32)
    slopes = measured_slopes.reshape(dirs, 2, rows, cols // 128, 128).transpose(0, 2, 3, 1, 4)
    slopes = slopes.reshape(dirs, rows, cols // 64, 128)
    fields, k0, k1 = pl.pallas_call(
        functools.partial(kernel, (dirs, lays, tiles, rows, cols, nl)),
        out_shape=(out,) + (jax.ShapeDtypeStruct((1, 128), F32),) * 2,
        in_specs=[pl.BlockSpec(memory_space=pltpu.HBM)] * 2 + [pl.BlockSpec(memory_space=pltpu.SMEM)] * 2,
        out_specs=(pl.BlockSpec(memory_space=pltpu.HBM),) + (pl.BlockSpec(memory_space=pltpu.VMEM),) * 2,
        scratch_shapes=[
            vm(dirs, 2 * st, rows + 4, 128),
            pltpu.VMEM((rows, 128 * st), jnp.int32),
            vm(2, st, 24, 128),
            vm(dirs, st, 48, 128),
            vm(2, lays, nt, 40, 128),
            vm(lays, nt, 40, 128),
            vm(lays, nt, 16, 128),
            vm(lays, nt, 8, 128),
            vm(2, nt, 16, 128),
            vm(nt, 56, 128),
            vm(3, lays, nt, 72, 128),
            vm(lays, nt, 72, 128),
            vm(5, 8, 128),
            vm(2, nt, 48, 128),
            vm(dirs, nt, 40, 128),
            vm(lays, nt, 32, 128),
            vm(3, lays, at * 2 * rows, 128),
            vm(16, 128),
            vm(g1 - 1, 128),
            vm(g2 - 1, 128),
            dma(2), dma(3), dma(3), dma(lays, 3), dma(lays, 3), dma(2, lays, 2), dma(2, lays, 2),
            dma(3), dma(3), dma(3), dma(2), dma(2),
        ],
        compiler_params=pltpu.CompilerParams(
            collective_id=0, has_side_effects=True, vmem_limit_bytes=56 * 1024 * 1024
        ),
    )(slopes, valid_mask, layer_offsets.transpose(1, 2, 0), reg_weight)
    part = jax.ShapeDtypeStruct((rows, cols // 128, 128), F32)
    whole = pl.BlockSpec(memory_space=pltpu.VMEM)
    est, res = pl.pallas_call(
        combine, out_shape=(part, part), in_specs=[whole] * 3, out_specs=(whole, whole)
    )(fields, k0, k1)
    return est.reshape(1, rows, cols), res.reshape(1, rows, cols)


def solution(mesh):
    return jax.shard_map(
        functools.partial(per_device, (mesh.shape["layer"], mesh.shape["tile"])),
        mesh=mesh,
        in_specs=(P(None, None, "tile", None), P("tile", None), P(), P()),
        out_specs=(P("layer", "tile", None), P("layer", "tile", None)),
        check_vma=False,
    )
```

```python
import functools

import jax
import jax.numpy as jnp
from jax import lax
from jax.experimental import pallas as pl
from jax.experimental.pallas import tpu as pltpu
from jax.sharding import PartitionSpec as P

MESH = pl.DeviceIdType.MESH
F32 = jnp.float32
HALO = 8
MARGIN = 64
ITERS = 2
REACH = 17


def kernel(
    cfg,
    slopes_hbm, mask_hbm, off, reg,
    fields, k0_ref, k1_ref,
    sl, mki, eb, q0, cb, sib, prv, nxt, ms, mb, xb, xw, sums, pb, qb, lb, ya, arsrc, ar1, ar2,
    in_sem, msend, mrecv, csend, crecv, hsend, hrecv, tsend, trecv, tlocal, asend, arecv,
):
    dirs, lays, tiles, rows, cols, nl = cfg
    two = 2 * rows
    width = cols // (2 * nl)
    at = width // 128
    nt = at + 1
    st = 2 * at + 2
    zs, xs = (2, 4) if tiles % 16 == 0 else (1, tiles // 2)
    g1 = nl * zs * 2
    g2 = tiles // (zs * 2)
    lay = lax.axis_index("layer")
    t = lax.axis_index("tile")
    chip = lax.div(t, 2)
    h = lax.rem(t, 2)
    chips = tiles // 2
    has_prev = chip > 0
    has_next = chip < chips - 1
    prev0 = 2 * chip - 2
    next0 = 2 * chip + 2
    lane = lax.broadcasted_iota(jnp.int32, (8, 128), 1)
    sub = lax.broadcasted_iota(jnp.int32, (8, 128), 0)
    zero = jnp.zeros((8, 128), F32)

    def rdma(src, dst, ss, rs, dev):
        return pltpu.make_async_remote_copy(
            src_ref=src, dst_ref=dst, send_sem=ss, recv_sem=rs, device_id=dev, device_id_type=MESH
        )

    def wait_bytes(ref, sem):
        pltpu.make_async_copy(ref, ref, sem).wait()

    barrier = pltpu.get_barrier_semaphore()

    def greet(dev):
        pl.semaphore_signal(barrier, inc=1, device_id=dev, device_id_type=MESH)

    other = 2 * chip + 1 - h

    @pl.when(has_prev)
    def _():
        greet((lay, prev0))
        greet((lay, prev0 + 1))

    @pl.when(has_next)
    def _():
        greet((lay, next0))
        greet((lay, next0 + 1))

    tx, tz, ty = lax.rem(chip, xs), lax.rem(lax.div(chip, xs), zs), lax.div(chip, xs * zs)
    me1 = (lay * zs + tz) * 2 + h
    me2 = ty * xs + tx

    def tile_at(y, z, x, core):
        return ((y * zs + z) * xs + x) * 2 + core

    def member1(d):
        index = lax.rem(me1 + d, g1)
        there = lax.div(index, 2 * zs)
        return (there, tile_at(ty, lax.rem(lax.div(index, 2), zs), tx, lax.rem(index, 2)))

    def member2(d):
        index = lax.rem(me2 + d, g2)
        return (lay, tile_at(lax.div(index, xs), tz, lax.rem(index, xs), h))

    def greet1(d, c):
        greet(member1(d))
        return c

    def greet2(d, c):
        greet(member2(d))
        return c

    lax.fori_loop(1, g1, greet1, 0, unroll=True)
    lax.fori_loop(1, g2, greet2, 0, unroll=True)

    span = 2 * width

    def mask_in(first, count, at_tile):
        src, dst = pl.ds(pl.multiple_of(first, 128), count), pl.ds(128 * at_tile, count)
        return pltpu.make_async_copy(mask_hbm.at[:, src], mki.at[:, dst], in_sem.at[0])

    def slopes_in(first, count, at_tile):
        src, dst = pl.ds(lax.div(first, 64), count // 64), pl.ds(2 * at_tile, count // 64)

        def one(i, c):
            pltpu.make_async_copy(slopes_hbm.at[:, i, src], sl.at[:, dst, i], in_sem.at[1]).start()
            return c

        lax.fori_loop(0, rows, one, 0)

    def slopes_wait(first, count, at_tile):
        dst = sl.at[:, pl.ds(2 * at_tile, count // 64), pl.ds(0, rows)]
        pltpu.make_async_copy(dst, dst, in_sem.at[1]).wait()

    def cases(act):
        @pl.when(lay == 0)
        def _():
            act(0, span + 128, 1)

        @pl.when(lay == nl - 1)
        def _():
            act(span * (nl - 1) - 128, span + 128, 0)

        @pl.when((lay > 0) & (lay < nl - 1))
        def _():
            act(span * lay - 128, span + 256, 0)

    cases(lambda *w: mask_in(*w).start())
    cases(slopes_in)

    @pl.when(lay == 0)
    def _():
        mki[:, 0:128] = jnp.zeros((rows, 128), jnp.int32)
        sl[:, 0:2, 0:rows] = jnp.zeros((dirs, 2, rows, 128), F32)

    @pl.when(lay == nl - 1)
    def _():
        mki[:, 128 * (st - 1) :] = jnp.zeros((rows, 128), jnp.int32)
        sl[:, 2 * st - 2 :, 0:rows] = jnp.zeros((dirs, 2, rows, 128), F32)

    sib[:, :, 0:8] = jnp.zeros((lays, nt, 8, 128), F32)
    sib[:, :, rows + 25 : 40] = jnp.zeros((lays, nt, 15 - rows, 128), F32)
    prv[:, :, HALO + 1 : 16] = jnp.zeros((lays, nt, 15 - HALO, 128), F32)
    mb[:, HALO + 1 + two + HALO :] = jnp.zeros((nt, 56 - two - 2 * HALO - 1, 128), F32)

    @pl.when(jnp.logical_not(has_prev))
    def _():
        prv[:, :, 0 : HALO + 1] = jnp.zeros((lays, nt, HALO + 1, 128), F32)
        mb[:, 0 : HALO + 1] = jnp.zeros((nt, HALO + 1, 128), F32)
        xb[0:2, :, :, 0:24] = jnp.zeros((2, lays, nt, 24, 128), F32)

    @pl.when(jnp.logical_not(has_next))
    def _():
        nxt[...] = jnp.zeros_like(nxt)
        mb[:, HALO + 1 + two : HALO + 1 + two + HALO] = jnp.zeros((nt, HALO, 128), F32)
        xb[0:2, :, :, 24 + two :] = jnp.zeros((2, lays, nt, 48 - two, 128), F32)

    eb[:, :, 0:8] = jnp.zeros((2, st, 8, 128), F32)
    eb[:, :, 16:24] = jnp.zeros((2, st, 8, 128), F32)
    q0[:, :, 0:16] = jnp.zeros((dirs, st, 16, 128), F32)
    q0[:, :, 32:48] = jnp.zeros((dirs, st, 16, 128), F32)
    cb[:, :, :, 0:8, :] = jnp.zeros((2, lays, nt, 8, 128), F32)

    cases(lambda *w: mask_in(*w).wait())
    bands = [slice(0, 8), slice(8, rows)]
    for k in range(2):
        for band in bands:
            turned = [
                pltpu.roll(mki[band, 128 * j : 128 * j + 128].astype(F32), MARGIN + HALO, 1)
                for j in range(at * k, at * k + nt + 1)
            ]
            keep = lane[: band.stop - band.start] < MARGIN + HALO
            for j in range(nt):
                ms[k, j, band, :] = jnp.where(keep, turned[j], turned[j + 1])
    mine = HALO + 1 + rows * h
    for j in range(nt):
        mb[j, pl.ds(mine, rows), :] = ms[h, j, 0:rows, :]
    def mask_sib():
        return rdma(
            ms.at[1 - h, :, pl.ds(0, rows)], mb.at[:, pl.ds(mine, rows)], msend.at[0], mrecv.at[0], (lay, other)
        )

    def mask_down(k):
        return rdma(
            ms.at[k, :, pl.ds(rows - HALO - 1, HALO + 1)], mb.at[:, pl.ds(0, HALO + 1)],
            msend.at[1 + k], mrecv.at[1], (lay, next0 + k),
        )

    def mask_up(k):
        return rdma(
            ms.at[k, :, pl.ds(0, HALO)], mb.at[:, pl.ds(HALO + 1 + two, HALO)],
            msend.at[1 + k], mrecv.at[2], (lay, prev0 + k),
        )

    sends_down = has_next & (h == 1)
    sends_up = has_prev & (h == 0)
    cases(slopes_wait)
    first_row = rows * t

    def own_adjoint(g, c):
        for band in bands:
            for j in range(st):
                at_cols = slice(128 * j, 128 * j + 128)
                m = mki[band, at_cols].astype(F32)
                u = m * sl[g, 2 * j, band, :]
                w = m * sl[g, 2 * j + 1, band, :]
                eb[0, j, 8 + band.start : 8 + band.stop, :] = u + w
                eb[1, j, 8 + band.start : 8 + band.stop, :] = u - w
        for rb in range(2):
            lo, up = 8 + 8 * rb, 7 + 8 * rb
            row_in = (first_row + 8 * rb + sub < rows * tiles).astype(F32)
            right = []
            for j in range(st):
                right.append(pltpu.roll(eb[0, j, up : up + 8, :] + eb[1, j, lo : lo + 8, :], 1, 1))
            for j in range(st):
                f = jnp.where(lane >= 1, right[j], right[max(j - 1, 0)])
                q = 0.5 * (f - eb[0, j, lo : lo + 8, :] - eb[1, j, up : up + 8, :])
                col_in = (span * lay - 128 + 128 * j + lane < cols).astype(F32)
                q0[g, j, 16 + 8 * rb : 24 + 8 * rb, :] = q * (row_in * col_in)
        return c

    lax.fori_loop(0, dirs, own_adjoint, 0)
    pl.semaphore_wait(
        barrier,
        2 * has_prev.astype(jnp.int32) + 2 * has_next.astype(jnp.int32) + (g1 - 1) + (g2 - 1),
    )

    mask_sib().start()

    @pl.when(sends_down)
    def _():
        mask_down(0).start()
        mask_down(1).start()

    @pl.when(sends_up)
    def _():
        mask_up(0).start()
        mask_up(1).start()


    def part_sib(l):
        return rdma(
            cb.at[1 - h, l, :, pl.ds(8, rows + 17)], sib.at[l, :, pl.ds(8, rows + 17)],
            csend.at[l, 0], crecv.at[l, 0], (lay, other),
        )

    def part_down(l, k):
        return rdma(
            cb.at[k, l, :, pl.ds(16 + rows, 9)], prv.at[l, :, pl.ds(0, 9)],
            csend.at[l, 1 + k], crecv.at[l, 1], (lay, next0 + k),
        )

    def part_up(l, k):
        return rdma(
            cb.at[k, l, :, pl.ds(8, 8)], nxt.at[l], csend.at[l, 1 + k], crecv.at[l, 2], (lay, prev0 + k)
        )

    def blocks(l, first):
        for k8 in range(2):
            at8 = pl.multiple_of(8 * (first + k8), 8)
            total = [[zero] * nt, [zero] * nt]
            for g in range(dirs):
                a, s = off[l, 0, g], MARGIN + off[l, 1, g]
                start = 8 + at8 - a
                turned = [pltpu.roll(q0[g, j, pl.ds(start, 8), :], s, 1) for j in range(st)]
                keep = lane < s
                for k in range(2):
                    for j in range(nt):
                        total[k][j] = total[k][j] + jnp.where(keep, turned[at * k + j], turned[at * k + j + 1])
            for k in range(2):
                for j in range(nt):
                    cb[k, l, j, pl.ds(8 + at8, 8), :] = total[k][j]

    def parts(step, c):
        l, last = lax.rem(step, lays), lax.div(step, lays)
        blocks(l, 2 * lax.rem(h + last, 2))

        @pl.when((last == 0) & sends_down)
        def _():
            part_down(l, 0).start()
            part_down(l, 1).start()

        @pl.when((last == 0) & sends_up)
        def _():
            part_up(l, 0).start()
            part_up(l, 1).start()

        @pl.when(last == 1)
        def _():
            part_sib(l).start()

        return c

    lax.fori_loop(0, 2 * lays, parts, 0)

    c0 = width * (2 * lay + h)
    xcol = [c0 - MARGIN + 128 * j + lane for j in range(nt)]
    x_in = [((v >= 0) & (v < cols)).astype(F32) for v in xcol]
    x_own = [((v >= c0) & (v < c0 + width)).astype(F32) for v in xcol]
    pcol = [c0 - MARGIN - HALO + 128 * j + lane for j in range(nt)]
    p_in = [((v >= 0) & (v < cols)).astype(F32) for v in pcol]
    p_own = [((v >= c0) & (v < c0 + width)).astype(F32) for v in pcol]
    chip_row = two * chip

    def row_inside(start):
        r = chip_row + start + sub
        return ((r >= 0) & (r < rows * tiles)).astype(F32)

    def halo_up(i, l):
        return rdma(
            xb.at[i, l, :, pl.ds(24, REACH)], xb.at[i, l, :, pl.ds(24 + two, REACH)],
            hsend.at[i, l, 0], hrecv.at[i, l, 0], (lay, prev0 + h),
        )

    def halo_down(i, l):
        return rdma(
            xb.at[i, l, :, pl.ds(24 + two - REACH, REACH)], xb.at[i, l, :, pl.ds(24 - REACH, REACH)],
            hsend.at[i, l, 1], hrecv.at[i, l, 1], (lay, next0 + h),
        )

    def send_halo(i, l):
        @pl.when(has_prev)
        def _():
            halo_up(i, l).start()

        @pl.when(has_next)
        def _():
            halo_down(i, l).start()

    def wait_halo(i, l):
        @pl.when(has_prev)
        def _():
            halo_down(i, l).wait_recv()

        @pl.when(has_next)
        def _():
            halo_up(i, l).wait_recv()

    def piece(i, l, half):
        src = ya.at[i, l, pl.ds(at * rows * half, at * rows)].reshape(rows, at, 128)
        dst = fields.at[i, :, pl.ds(at * (2 * lay + h), at)]
        return src, dst

    def send_pieces(i, l):
        for half in range(2):
            src, dst = piece(i, l, half)
            here = (l == lay) & (half == h)

            @pl.when(here)
            def _():
                pltpu.make_async_copy(src, dst, tlocal.at[i]).start()

            @pl.when(jnp.logical_not(here))
            def _():
                rdma(src, dst, tsend.at[i], trecv.at[i], (l, 2 * chip + half)).start()

    def stage(i, l, rb, value):
        turned = [pltpu.roll(v, MARGIN, 1) for v in value]
        for k in range(at):
            ya[i, l, pl.ds(at * 8 * rb + k, 8, stride=at), :] = jnp.where(lane < MARGIN, turned[k], turned[k + 1])

    def finish_b(l, acc):
        part_sib(l).wait_recv()

        @pl.when(has_prev)
        def _():
            part_down(l, 0).wait_recv()

        @pl.when(has_next)
        def _():
            part_up(l, 0).wait_recv()

        for rb in range(two // 8):
            value = []
            for j in range(nt):
                v = cb[h, l, j, pl.ds(16 + 8 * rb - rows * h, 8), :]
                v = v + sib[l, j, pl.ds(16 + 8 * rb - rows * (1 - h), 8), :]
                if rb < 2:
                    v = v + prv[l, j, 8 * rb : 8 * rb + 8, :]
                if rb == two // 8 - 1:
                    v = v + nxt[l, j]
                v = v * x_in[j]
                acc = acc + x_own[j] * (v * v)
                xb[0, l, j, 24 + 8 * rb : 32 + 8 * rb, :] = v
                value.append(v)
            stage(0, l, rb, value)
        send_halo(0, l)
        return acc

    sums[0] = lax.fori_loop(0, lays, finish_b, zero)

    mask_sib().wait_recv()

    @pl.when(has_prev)
    def _():
        mask_down(0).wait_recv()

    @pl.when(has_next)
    def _():
        mask_up(0).wait_recv()

    def beside(value):
        n = len(value)
        r = [pltpu.roll(v, 1, 1) for v in value]
        l = [pltpu.roll(v, 127, 1) for v in value]
        left = [jnp.where(lane >= 1, r[j], r[(j - 1) % n]) for j in range(n)]
        right = [jnp.where(lane < 127, l[j], l[(j + 1) % n]) for j in range(n)]
        return left, right

    def front(i):
        def smooth(l, acc):
            wait_halo(i, l)
            for j in range(nt):
                xw[l, j] = xb[i, l, j]
            part = zero
            for rb in range(4):
                row = -1 + 8 * rb
                mid = [xb[i, l, j, 24 + row : 32 + row, :] for j in range(nt)]
                left, right = beside(mid)
                inside = row_inside(row)
                own = ((row + sub >= 0) & (row + sub < two)).astype(F32)
                for j in range(nt):
                    v = 4.0 * mid[j] - xb[i, l, j, 23 + row : 31 + row, :] - xb[i, l, j, 25 + row : 33 + row, :]
                    v = (v - left[j] - right[j]) * (inside * x_in[j])
                    lb[l, j, 8 * rb : 8 * rb + 8, :] = v
                    part = part + (own * x_own[j]) * (v * v)
            return acc + reg[l] * part

        energy = lax.fori_loop(0, lays, smooth, zero)

        def give(l, c):
            send_pieces(i, l)
            return c

        lax.fori_loop(0, lays, give, 0)

        def project(g, acc):
            for rb in range(6):
                total = [zero] * nt
                for l in range(lays):
                    a, s = off[l, 0, g], HALO - off[l, 1, g]
                    start = 15 + 8 * rb + a
                    turned = [pltpu.roll(xw[l, j, pl.ds(start, 8), :], s, 1) for j in range(nt)]
                    keep = lane >= s
                    total = [total[j] + jnp.where(keep, turned[j], turned[(j - 1) % nt]) for j in range(nt)]
                inside = row_inside(8 * rb - 9)
                total = [total[j] * (inside * p_in[j]) for j in range(nt)]
                turned = [pltpu.roll(v, 127, 1) for v in total]
                for j in range(nt):
                    pb[0, j, 8 * rb : 8 * rb + 8, :] = total[j]
                    pb[1, j, 8 * rb : 8 * rb + 8, :] = jnp.where(lane < 127, turned[j], turned[(j + 1) % nt])
            for rb in range(5):
                up, lo, dn = 8 * rb, 8 * rb + 1, 8 * rb + 2
                turned, rest = [], []
                inside = row_inside(8 * rb - 8)
                for j in range(nt):
                    m_lo, m_up = mb[j, lo : lo + 8, :], mb[j, up : up + 8, :]
                    p_lo, r_lo = pb[0, j, lo : lo + 8, :], pb[1, j, lo : lo + 8, :]
                    e1 = m_lo * (pb[1, j, dn : dn + 8, :] - p_lo)
                    e2 = m_lo * (r_lo - pb[0, j, dn : dn + 8, :])
                    e1_up = m_up * (r_lo - pb[0, j, up : up + 8, :])
                    e2_up = m_up * (pb[1, j, up : up + 8, :] - p_lo)
                    if 1 <= rb <= two // 8:
                        acc = acc + (0.5 * p_own[j]) * (e1 * e1 + e2 * e2)
                    turned.append(pltpu.roll(e1_up + e2, 1, 1))
                    rest.append(e1 + e2_up)
                for j in range(nt):
                    f = jnp.where(lane >= 1, turned[j], turned[(j - 1) % nt])
                    qb[g, j, 8 * rb : 8 * rb + 8, :] = (f - rest[j]) * (0.5 * inside * p_in[j])
            return acc

        return lax.fori_loop(0, dirs, project, energy)

    def back(i):
        def layer(l, acc):
            for rb in range(two // 8):
                total = [zero] * nt
                for g in range(dirs):
                    a, s = off[l, 0, g], lax.rem(120 + off[l, 1, g], 128)
                    start = 8 + 8 * rb - a
                    turned = [pltpu.roll(qb[g, j, pl.ds(start, 8), :], s, 1) for j in range(nt)]
                    keep = lane < 120 + off[l, 1, g]
                    total = [total[j] + jnp.where(keep, turned[j], turned[(j + 1) % nt]) for j in range(nt)]
                lo = 8 * rb + 1
                mid = [lb[l, j, lo : lo + 8, :] for j in range(nt)]
                left, right = beside(mid)
                value = []
                for j in range(nt):
                    v = 4.0 * mid[j] - lb[l, j, lo - 1 : lo + 7, :] - lb[l, j, lo + 1 : lo + 9, :] - left[j] - right[j]
                    v = (total[j] + reg[l] * v) * x_in[j]
                    acc = acc + x_own[j] * (v * v)
                    xb[i, l, j, 24 + 8 * rb : 32 + 8 * rb, :] = v
                    value.append(v)
                stage(i, l, rb, value)

            @pl.when(i < ITERS)
            def _():
                send_halo(i, l)

            @pl.when(i == ITERS)
            def _():
                send_pieces(i, l)

            return acc

        return lax.fori_loop(0, lays, layer, zero)

    lane1 = lane[0:1]

    def whole(v):
        return jnp.sum(jnp.sum(v, axis=0, keepdims=True), axis=1, keepdims=True)

    def exchange(stage_id, slots, count, member):
        def one(d, c):
            rdma(
                arsrc.at[pl.ds(8 * stage_id, 1)], slots.at[pl.ds(count - 1 - d, 1)],
                asend.at[stage_id], arecv.at[stage_id], member(d),
            ).start()
            return c

        lax.fori_loop(1, count, one, 0, unroll=True)

    def apply(i, c):
        sums[1 + i] = front(i)

        @pl.when(i == ITERS - 1)
        def _():
            packed = jnp.zeros((1, 128), F32)
            for k, n in enumerate((0, 1, 3, 2)):
                packed = jnp.where(lane1 == k, whole(sums[n]), packed)
            arsrc[0:1, :] = packed
            exchange(0, ar2, g2, member2)

        sums[3 + i] = back(i + 1)
        return c

    lax.fori_loop(0, ITERS, apply, 0)
    wait_bytes(ar2, arecv.at[0])
    arsrc[8:9, :] = arsrc[0:1, :] + jnp.sum(ar2[...], axis=0, keepdims=True)
    exchange(1, ar1, g1, member1)
    wait_bytes(ar1, arecv.at[1])
    total = arsrc[8:9, :] + jnp.sum(ar1[...], axis=0, keepdims=True)
    bb, e0, yy, e1 = (jnp.sum(jnp.where(lane1 == k, total, 0.0), axis=1, keepdims=True) for k in range(4))
    a0 = bb / e0
    rr = a0 * a0 * yy - bb
    beta = rr / bb
    grown = 1.0 + beta
    a1 = rr / (grown * grown * e0 - 2.0 * a0 * grown * yy + a0 * a0 * e1)
    k0_ref[...] = jnp.broadcast_to(a0 + a1 * grown, (1, 128))
    k1_ref[...] = jnp.broadcast_to(a0 * a1, (1, 128))

    for i in range(3):
        wait_bytes(fields.at[i, :, pl.ds(0, at * (2 * nl - 1))], trecv.at[i])
        src, dst = piece(i, 0, 0)
        pltpu.make_async_copy(src, dst, tlocal.at[i]).wait()

    mask_sib().wait_send()

    @pl.when(sends_down)
    def _():
        mask_down(0).wait_send()
        mask_down(1).wait_send()

    @pl.when(sends_up)
    def _():
        mask_up(0).wait_send()
        mask_up(1).wait_send()

    def drain(l, c):
        part_sib(l).wait_send()

        @pl.when(sends_down)
        def _():
            part_down(l, 0).wait_send()
            part_down(l, 1).wait_send()

        @pl.when(sends_up)
        def _():
            part_up(l, 0).wait_send()
            part_up(l, 1).wait_send()

        for i in range(ITERS):

            @pl.when(has_prev)
            def _():
                halo_up(i, l).wait_send()

            @pl.when(has_next)
            def _():
                halo_down(i, l).wait_send()

        return c

    lax.fori_loop(0, lays, drain, 0)
    for i in range(3):
        wait_bytes(fields.at[i, :, pl.ds(0, at * (2 * nl - 1))], tsend.at[i])
    wait_bytes(ar2, asend.at[0])
    wait_bytes(ar1, asend.at[1])


def combine(fields, k0, k1, est, res):
    a, c = k0[...], k1[...]
    for r in range(fields.shape[1]):
        b, y1, y2 = fields[0, r], fields[1, r], fields[2, r]
        est[r] = a * b - c * y1
        res[r] = b - a * y1 + c * y2


def per_device(shape, measured_slopes, valid_mask, layer_offsets, reg_weight):
    nl, tiles = shape
    dirs, _, rows, cols = measured_slopes.shape
    lays = layer_offsets.shape[1]
    width = cols // (2 * nl)
    at = width // 128
    nt, st = at + 1, 2 * at + 2
    zs = 2 if tiles % 16 == 0 else 1
    g1, g2 = nl * zs * 2, tiles // (zs * 2)
    vm = lambda *s: pltpu.VMEM(s, F32)
    dma = lambda *s: pltpu.SemaphoreType.DMA(s)
    out = jax.ShapeDtypeStruct((3, rows, cols // 128, 128), F32)
    slopes = measured_slopes.reshape(dirs, 2, rows, cols // 128, 128).transpose(0, 2, 3, 1, 4)
    slopes = slopes.reshape(dirs, rows, cols // 64, 128)
    fields, k0, k1 = pl.pallas_call(
        functools.partial(kernel, (dirs, lays, tiles, rows, cols, nl)),
        out_shape=(out,) + (jax.ShapeDtypeStruct((1, 128), F32),) * 2,
        in_specs=[pl.BlockSpec(memory_space=pltpu.HBM)] * 2 + [pl.BlockSpec(memory_space=pltpu.SMEM)] * 2,
        out_specs=(pl.BlockSpec(memory_space=pltpu.HBM),) + (pl.BlockSpec(memory_space=pltpu.VMEM),) * 2,
        scratch_shapes=[
            vm(dirs, 2 * st, rows + 4, 128),
            pltpu.VMEM((rows, 128 * st), jnp.int32),
            vm(2, st, 24, 128),
            vm(dirs, st, 48, 128),
            vm(2, lays, nt, 40, 128),
            vm(lays, nt, 40, 128),
            vm(lays, nt, 16, 128),
            vm(lays, nt, 8, 128),
            vm(2, nt, 16, 128),
            vm(nt, 56, 128),
            vm(3, lays, nt, 72, 128),
            vm(lays, nt, 72, 128),
            vm(5, 8, 128),
            vm(2, nt, 48, 128),
            vm(dirs, nt, 40, 128),
            vm(lays, nt, 32, 128),
            vm(3, lays, at * 2 * rows, 128),
            vm(16, 128),
            vm(g1 - 1, 128),
            vm(g2 - 1, 128),
            dma(2), dma(3), dma(3), dma(lays, 3), dma(lays, 3), dma(2, lays, 2), dma(2, lays, 2),
            dma(3), dma(3), dma(3), dma(2), dma(2),
        ],
        compiler_params=pltpu.CompilerParams(
            collective_id=0, has_side_effects=True, vmem_limit_bytes=56 * 1024 * 1024
        ),
    )(slopes, valid_mask, layer_offsets.transpose(1, 2, 0), reg_weight)
    part = jax.ShapeDtypeStruct((rows, cols // 128, 128), F32)
    whole = pl.BlockSpec(memory_space=pltpu.VMEM)
    est, res = pl.pallas_call(
        combine, out_shape=(part, part), in_specs=[whole] * 3, out_specs=(whole, whole)
    )(fields, k0, k1)
    return est.reshape(1, rows, cols), res.reshape(1, rows, cols)


def solution(mesh):
    return jax.shard_map(
        functools.partial(per_device, (mesh.shape["layer"], mesh.shape["tile"])),
        mesh=mesh,
        in_specs=(P(None, None, "tile", None), P("tile", None), P(), P()),
        out_specs=(P("layer", "tile", None), P("layer", "tile", None)),
        check_vma=False,
    )
```

```python
import functools

import jax
import jax.numpy as jnp
from jax import lax
from jax.experimental import pallas as pl
from jax.experimental.pallas import tpu as pltpu
from jax.sharding import PartitionSpec as P

MESH = pl.DeviceIdType.MESH
F32 = jnp.float32
HALO = 8
MARGIN = 64
ITERS = 2
REACH = 17


def kernel(
    cfg,
    slopes_hbm, mask_hbm, off, reg,
    fields, k0_ref, k1_ref,
    sl, mki, eb, q0, cb, sib, prv, nxt, ms, mb, xb, xw, sums, pb, qb, lb, ya, arsrc, ar1, ar2,
    in_sem, msend, mrecv, csend, crecv, hsend, hrecv, tsend, trecv, tlocal, asend, arecv,
):
    dirs, lays, tiles, rows, cols, nl = cfg
    two = 2 * rows
    width = cols // (2 * nl)
    at = width // 128
    nt = at + 1
    st = 2 * at + 2
    zs, xs = (2, 4) if tiles % 16 == 0 else (1, tiles // 2)
    g1 = nl * zs * 2
    g2 = tiles // (zs * 2)
    lay = lax.axis_index("layer")
    t = lax.axis_index("tile")
    chip = lax.div(t, 2)
    h = lax.rem(t, 2)
    chips = tiles // 2
    has_prev = chip > 0
    has_next = chip < chips - 1
    prev0 = 2 * chip - 2
    next0 = 2 * chip + 2
    lane = lax.broadcasted_iota(jnp.int32, (8, 128), 1)
    sub = lax.broadcasted_iota(jnp.int32, (8, 128), 0)
    zero = jnp.zeros((8, 128), F32)

    def rdma(src, dst, ss, rs, dev):
        return pltpu.make_async_remote_copy(
            src_ref=src, dst_ref=dst, send_sem=ss, recv_sem=rs, device_id=dev, device_id_type=MESH
        )

    def wait_bytes(ref, sem):
        pltpu.make_async_copy(ref, ref, sem).wait()

    barrier = pltpu.get_barrier_semaphore()

    def greet(dev):
        pl.semaphore_signal(barrier, inc=1, device_id=dev, device_id_type=MESH)

    other = 2 * chip + 1 - h

    @pl.when(has_prev)
    def _():
        greet((lay, prev0))
        greet((lay, prev0 + 1))

    @pl.when(has_next)
    def _():
        greet((lay, next0))
        greet((lay, next0 + 1))

    tx, tz, ty = lax.rem(chip, xs), lax.rem(lax.div(chip, xs), zs), lax.div(chip, xs * zs)
    me1 = (lay * zs + tz) * 2 + h
    me2 = ty * xs + tx

    def tile_at(y, z, x, core):
        return ((y * zs + z) * xs + x) * 2 + core

    def member1(d):
        index = lax.rem(me1 + d, g1)
        there = lax.div(index, 2 * zs)
        return (there, tile_at(ty, lax.rem(lax.div(index, 2), zs), tx, lax.rem(index, 2)))

    def member2(d):
        index = lax.rem(me2 + d, g2)
        return (lay, tile_at(lax.div(index, xs), tz, lax.rem(index, xs), h))

    def greet1(d, c):
        greet(member1(d))
        return c

    def greet2(d, c):
        greet(member2(d))
        return c

    lax.fori_loop(1, g1, greet1, 0, unroll=True)
    lax.fori_loop(1, g2, greet2, 0, unroll=True)

    span = 2 * width

    def mask_in(first, count, at_tile):
        src, dst = pl.ds(pl.multiple_of(first, 128), count), pl.ds(128 * at_tile, count)
        return pltpu.make_async_copy(mask_hbm.at[:, src], mki.at[:, dst], in_sem.at[0])

    def slopes_in(first, count, at_tile):
        src, dst = pl.ds(lax.div(first, 64), count // 64), pl.ds(2 * at_tile, count // 64)

        def one(i, c):
            pltpu.make_async_copy(slopes_hbm.at[:, i, src], sl.at[:, dst, i], in_sem.at[1]).start()
            return c

        lax.fori_loop(0, rows, one, 0)

    def slopes_wait(first, count, at_tile):
        dst = sl.at[:, pl.ds(2 * at_tile, count // 64), pl.ds(0, rows)]
        pltpu.make_async_copy(dst, dst, in_sem.at[1]).wait()

    def cases(act):
        @pl.when(lay == 0)
        def _():
            act(0, span + 128, 1)

        @pl.when(lay == nl - 1)
        def _():
            act(span * (nl - 1) - 128, span + 128, 0)

        @pl.when((lay > 0) & (lay < nl - 1))
        def _():
            act(span * lay - 128, span + 256, 0)

    cases(lambda *w: mask_in(*w).start())
    cases(slopes_in)

    @pl.when(lay == 0)
    def _():
        mki[:, 0:128] = jnp.zeros((rows, 128), jnp.int32)
        sl[:, 0:2, 0:rows] = jnp.zeros((dirs, 2, rows, 128), F32)

    @pl.when(lay == nl - 1)
    def _():
        mki[:, 128 * (st - 1) :] = jnp.zeros((rows, 128), jnp.int32)
        sl[:, 2 * st - 2 :, 0:rows] = jnp.zeros((dirs, 2, rows, 128), F32)

    sib[:, :, 0:8] = jnp.zeros((lays, nt, 8, 128), F32)
    sib[:, :, rows + 25 : 40] = jnp.zeros((lays, nt, 15 - rows, 128), F32)
    prv[:, :, HALO + 1 : 16] = jnp.zeros((lays, nt, 15 - HALO, 128), F32)
    mb[:, HALO + 1 + two + HALO :] = jnp.zeros((nt, 56 - two - 2 * HALO - 1, 128), F32)

    @pl.when(jnp.logical_not(has_prev))
    def _():
        prv[:, :, 0 : HALO + 1] = jnp.zeros((lays, nt, HALO + 1, 128), F32)
        mb[:, 0 : HALO + 1] = jnp.zeros((nt, HALO + 1, 128), F32)
        xb[0:2, :, :, 0:24] = jnp.zeros((2, lays, nt, 24, 128), F32)

    @pl.when(jnp.logical_not(has_next))
    def _():
        nxt[...] = jnp.zeros_like(nxt)
        mb[:, HALO + 1 + two : HALO + 1 + two + HALO] = jnp.zeros((nt, HALO, 128), F32)
        xb[0:2, :, :, 24 + two :] = jnp.zeros((2, lays, nt, 48 - two, 128), F32)

    eb[:, :, 0:8] = jnp.zeros((2, st, 8, 128), F32)
    eb[:, :, 16:24] = jnp.zeros((2, st, 8, 128), F32)
    q0[:, :, 0:16] = jnp.zeros((dirs, st, 16, 128), F32)
    q0[:, :, 32:48] = jnp.zeros((dirs, st, 16, 128), F32)
    cb[:, :, :, 0:8, :] = jnp.zeros((2, lays, nt, 8, 128), F32)

    cases(lambda *w: mask_in(*w).wait())
    bands = [slice(0, 8), slice(8, rows)]
    for k in range(2):
        for band in bands:
            turned = [
                pltpu.roll(mki[band, 128 * j : 128 * j + 128].astype(F32), MARGIN + HALO, 1)
                for j in range(at * k, at * k + nt + 1)
            ]
            keep = lane[: band.stop - band.start] < MARGIN + HALO
            for j in range(nt):
                ms[k, j, band, :] = jnp.where(keep, turned[j], turned[j + 1])
    mine = HALO + 1 + rows * h
    for j in range(nt):
        mb[j, pl.ds(mine, rows), :] = ms[h, j, 0:rows, :]
    def mask_sib():
        return rdma(
            ms.at[1 - h, :, pl.ds(0, rows)], mb.at[:, pl.ds(mine, rows)], msend.at[0], mrecv.at[0], (lay, other)
        )

    def mask_down(k):
        return rdma(
            ms.at[k, :, pl.ds(rows - HALO - 1, HALO + 1)], mb.at[:, pl.ds(0, HALO + 1)],
            msend.at[1 + k], mrecv.at[1], (lay, next0 + k),
        )

    def mask_up(k):
        return rdma(
            ms.at[k, :, pl.ds(0, HALO)], mb.at[:, pl.ds(HALO + 1 + two, HALO)],
            msend.at[1 + k], mrecv.at[2], (lay, prev0 + k),
        )

    sends_down = has_next & (h == 1)
    sends_up = has_prev & (h == 0)
    cases(slopes_wait)
    first_row = rows * t

    def own_adjoint(g, c):
        for band in bands:
            for j in range(st):
                at_cols = slice(128 * j, 128 * j + 128)
                m = mki[band, at_cols].astype(F32)
                u = m * sl[g, 2 * j, band, :]
                w = m * sl[g, 2 * j + 1, band, :]
                eb[0, j, 8 + band.start : 8 + band.stop, :] = u + w
                eb[1, j, 8 + band.start : 8 + band.stop, :] = u - w
        for rb in range(2):
            lo, up = 8 + 8 * rb, 7 + 8 * rb
            row_in = (first_row + 8 * rb + sub < rows * tiles).astype(F32)
            right = []
            for j in range(st):
                right.append(pltpu.roll(eb[0, j, up : up + 8, :] + eb[1, j, lo : lo + 8, :], 1, 1))
            for j in range(st):
                f = jnp.where(lane >= 1, right[j], right[max(j - 1, 0)])
                q = 0.5 * (f - eb[0, j, lo : lo + 8, :] - eb[1, j, up : up + 8, :])
                col_in = (span * lay - 128 + 128 * j + lane < cols).astype(F32)
                q0[g, j, 16 + 8 * rb : 24 + 8 * rb, :] = q * (row_in * col_in)
        return c

    lax.fori_loop(0, dirs, own_adjoint, 0)
    pl.semaphore_wait(
        barrier,
        2 * has_prev.astype(jnp.int32) + 2 * has_next.astype(jnp.int32) + (g1 - 1) + (g2 - 1),
    )

    mask_sib().start()

    @pl.when(sends_down)
    def _():
        mask_down(0).start()
        mask_down(1).start()

    @pl.when(sends_up)
    def _():
        mask_up(0).start()
        mask_up(1).start()


    def part_sib(l):
        return rdma(
            cb.at[1 - h, l, :, pl.ds(8, rows + 17)], sib.at[l, :, pl.ds(8, rows + 17)],
            csend.at[l, 0], crecv.at[l, 0], (lay, other),
        )

    def part_down(l, k):
        return rdma(
            cb.at[k, l, :, pl.ds(16 + rows, 9)], prv.at[l, :, pl.ds(0, 9)],
            csend.at[l, 1 + k], crecv.at[l, 1], (lay, next0 + k),
        )

    def part_up(l, k):
        return rdma(
            cb.at[k, l, :, pl.ds(8, 8)], nxt.at[l], csend.at[l, 1 + k], crecv.at[l, 2], (lay, prev0 + k)
        )

    def blocks(l, first):
        for k8 in range(2):
            at8 = pl.multiple_of(8 * (first + k8), 8)
            total = [[zero] * nt, [zero] * nt]
            for g in range(dirs):
                a, s = off[l, 0, g], MARGIN + off[l, 1, g]
                start = 8 + at8 - a
                turned = [pltpu.roll(q0[g, j, pl.ds(start, 8), :], s, 1) for j in range(st)]
                keep = lane < s
                for k in range(2):
                    for j in range(nt):
                        total[k][j] = total[k][j] + jnp.where(keep, turned[at * k + j], turned[at * k + j + 1])
            for k in range(2):
                for j in range(nt):
                    cb[k, l, j, pl.ds(8 + at8, 8), :] = total[k][j]

    def parts(step, c):
        l, last = lax.rem(step, lays), lax.div(step, lays)
        blocks(l, 2 * lax.rem(h + last, 2))

        @pl.when((last == 0) & sends_down)
        def _():
            part_down(l, 0).start()
            part_down(l, 1).start()

        @pl.when((last == 0) & sends_up)
        def _():
            part_up(l, 0).start()
            part_up(l, 1).start()

        @pl.when(last == 1)
        def _():
            part_sib(l).start()

        return c

    lax.fori_loop(0, 2 * lays, parts, 0)

    c0 = width * (2 * lay + h)
    xcol = [c0 - MARGIN + 128 * j + lane for j in range(nt)]
    x_in = [((v >= 0) & (v < cols)).astype(F32) for v in xcol]
    x_own = [((v >= c0) & (v < c0 + width)).astype(F32) for v in xcol]
    pcol = [c0 - MARGIN - HALO + 128 * j + lane for j in range(nt)]
    p_in = [((v >= 0) & (v < cols)).astype(F32) for v in pcol]
    p_own = [((v >= c0) & (v < c0 + width)).astype(F32) for v in pcol]
    chip_row = two * chip

    def row_inside(start):
        r = chip_row + start + sub
        return ((r >= 0) & (r < rows * tiles)).astype(F32)

    def halo_up(i, l):
        return rdma(
            xb.at[i, l, :, pl.ds(24, REACH)], xb.at[i, l, :, pl.ds(24 + two, REACH)],
            hsend.at[i, l, 0], hrecv.at[i, l, 0], (lay, prev0 + h),
        )

    def halo_down(i, l):
        return rdma(
            xb.at[i, l, :, pl.ds(24 + two - REACH, REACH)], xb.at[i, l, :, pl.ds(24 - REACH, REACH)],
            hsend.at[i, l, 1], hrecv.at[i, l, 1], (lay, next0 + h),
        )

    def send_halo(i, l):
        @pl.when(has_prev)
        def _():
            halo_up(i, l).start()

        @pl.when(has_next)
        def _():
            halo_down(i, l).start()

    def wait_halo(i, l):
        @pl.when(has_prev)
        def _():
            halo_down(i, l).wait_recv()

        @pl.when(has_next)
        def _():
            halo_up(i, l).wait_recv()

    def piece(i, l, half):
        src = ya.at[i, l, pl.ds(at * rows * half, at * rows)].reshape(rows, at, 128)
        dst = fields.at[i, :, pl.ds(at * (2 * lay + h), at)]
        return src, dst

    def send_pieces(i, l):
        for half in range(2):
            src, dst = piece(i, l, half)
            here = (l == lay) & (half == h)

            @pl.when(here)
            def _():
                pltpu.make_async_copy(src, dst, tlocal.at[i]).start()

            @pl.when(jnp.logical_not(here))
            def _():
                rdma(src, dst, tsend.at[i], trecv.at[i], (l, 2 * chip + half)).start()

    def stage(i, l, rb, value):
        turned = [pltpu.roll(v, MARGIN, 1) for v in value]
        for k in range(at):
            ya[i, l, pl.ds(at * 8 * rb + k, 8, stride=at), :] = jnp.where(lane < MARGIN, turned[k], turned[k + 1])

    def finish_b(l, acc):
        part_sib(l).wait_recv()

        @pl.when(has_prev)
        def _():
            part_down(l, 0).wait_recv()

        @pl.when(has_next)
        def _():
            part_up(l, 0).wait_recv()

        for rb in range(two // 8):
            value = []
            for j in range(nt):
                v = cb[h, l, j, pl.ds(16 + 8 * rb - rows * h, 8), :]
                v = v + sib[l, j, pl.ds(16 + 8 * rb - rows * (1 - h), 8), :]
                if rb < 2:
                    v = v + prv[l, j, 8 * rb : 8 * rb + 8, :]
                if rb == two // 8 - 1:
                    v = v + nxt[l, j]
                v = v * x_in[j]
                acc = acc + x_own[j] * (v * v)
                xb[0, l, j, 24 + 8 * rb : 32 + 8 * rb, :] = v
                value.append(v)
            stage(0, l, rb, value)
        send_halo(0, l)
        return acc

    sums[0] = lax.fori_loop(0, lays, finish_b, zero)

    mask_sib().wait_recv()

    @pl.when(has_prev)
    def _():
        mask_down(0).wait_recv()

    @pl.when(has_next)
    def _():
        mask_up(0).wait_recv()

    def beside(value):
        n = len(value)
        r = [pltpu.roll(v, 1, 1) for v in value]
        l = [pltpu.roll(v, 127, 1) for v in value]
        left = [jnp.where(lane >= 1, r[j], r[(j - 1) % n]) for j in range(n)]
        right = [jnp.where(lane < 127, l[j], l[(j + 1) % n]) for j in range(n)]
        return left, right

    def front(i):
        def smooth(l, acc):
            wait_halo(i, l)

            @pl.when(l >= lays // 2)
            def _():
                send_pieces(i, l - lays // 2)

            for j in range(nt):
                xw[l, j] = xb[i, l, j]
            part = zero
            for rb in range(4):
                row = -1 + 8 * rb
                mid = [xb[i, l, j, 24 + row : 32 + row, :] for j in range(nt)]
                left, right = beside(mid)
                inside = row_inside(row)
                own = ((row + sub >= 0) & (row + sub < two)).astype(F32)
                for j in range(nt):
                    v = 4.0 * mid[j] - xb[i, l, j, 23 + row : 31 + row, :] - xb[i, l, j, 25 + row : 33 + row, :]
                    v = (v - left[j] - right[j]) * (inside * x_in[j])
                    lb[l, j, 8 * rb : 8 * rb + 8, :] = v
                    part = part + (own * x_own[j]) * (v * v)
            return acc + reg[l] * part

        energy = lax.fori_loop(0, lays, smooth, zero)

        def give(l, c):
            send_pieces(i, l)
            return c

        lax.fori_loop(lays // 2, lays, give, 0)

        def project(g, acc):
            for rb in range(6):
                total = [zero] * nt
                for l in range(lays):
                    a, s = off[l, 0, g], HALO - off[l, 1, g]
                    start = 15 + 8 * rb + a
                    turned = [pltpu.roll(xw[l, j, pl.ds(start, 8), :], s, 1) for j in range(nt)]
                    keep = lane >= s
                    total = [total[j] + jnp.where(keep, turned[j], turned[(j - 1) % nt]) for j in range(nt)]
                inside = row_inside(8 * rb - 9)
                total = [total[j] * (inside * p_in[j]) for j in range(nt)]
                turned = [pltpu.roll(v, 127, 1) for v in total]
                for j in range(nt):
                    pb[0, j, 8 * rb : 8 * rb + 8, :] = total[j]
                    pb[1, j, 8 * rb : 8 * rb + 8, :] = jnp.where(lane < 127, turned[j], turned[(j + 1) % nt])
            for rb in range(5):
                up, lo, dn = 8 * rb, 8 * rb + 1, 8 * rb + 2
                turned, rest = [], []
                inside = row_inside(8 * rb - 8)
                for j in range(nt):
                    m_lo, m_up = mb[j, lo : lo + 8, :], mb[j, up : up + 8, :]
                    p_lo, r_lo = pb[0, j, lo : lo + 8, :], pb[1, j, lo : lo + 8, :]
                    e1 = m_lo * (pb[1, j, dn : dn + 8, :] - p_lo)
                    e2 = m_lo * (r_lo - pb[0, j, dn : dn + 8, :])
                    e1_up = m_up * (r_lo - pb[0, j, up : up + 8, :])
                    e2_up = m_up * (pb[1, j, up : up + 8, :] - p_lo)
                    if 1 <= rb <= two // 8:
                        acc = acc + (0.5 * p_own[j]) * (e1 * e1 + e2 * e2)
                    turned.append(pltpu.roll(e1_up + e2, 1, 1))
                    rest.append(e1 + e2_up)
                for j in range(nt):
                    f = jnp.where(lane >= 1, turned[j], turned[(j - 1) % nt])
                    qb[g, j, 8 * rb : 8 * rb + 8, :] = (f - rest[j]) * (0.5 * inside * p_in[j])
            return acc

        return lax.fori_loop(0, dirs, project, energy)

    def back(i):
        def layer(l, acc):
            for rb in range(two // 8):
                total = [zero] * nt
                for g in range(dirs):
                    a, s = off[l, 0, g], lax.rem(120 + off[l, 1, g], 128)
                    start = 8 + 8 * rb - a
                    turned = [pltpu.roll(qb[g, j, pl.ds(start, 8), :], s, 1) for j in range(nt)]
                    keep = lane < 120 + off[l, 1, g]
                    total = [total[j] + jnp.where(keep, turned[j], turned[(j + 1) % nt]) for j in range(nt)]
                lo = 8 * rb + 1
                mid = [lb[l, j, lo : lo + 8, :] for j in range(nt)]
                left, right = beside(mid)
                value = []
                for j in range(nt):
                    v = 4.0 * mid[j] - lb[l, j, lo - 1 : lo + 7, :] - lb[l, j, lo + 1 : lo + 9, :] - left[j] - right[j]
                    v = (total[j] + reg[l] * v) * x_in[j]
                    acc = acc + x_own[j] * (v * v)
                    xb[i, l, j, 24 + 8 * rb : 32 + 8 * rb, :] = v
                    value.append(v)
                stage(i, l, rb, value)

            @pl.when(i < ITERS)
            def _():
                send_halo(i, l)

            @pl.when(i == ITERS)
            def _():
                send_pieces(i, l)

            return acc

        return lax.fori_loop(0, lays, layer, zero)

    lane1 = lane[0:1]

    def whole(v):
        return jnp.sum(jnp.sum(v, axis=0, keepdims=True), axis=1, keepdims=True)

    def exchange(stage_id, slots, count, member):
        def one(d, c):
            rdma(
                arsrc.at[pl.ds(8 * stage_id, 1)], slots.at[pl.ds(count - 1 - d, 1)],
                asend.at[stage_id], arecv.at[stage_id], member(d),
            ).start()
            return c

        lax.fori_loop(1, count, one, 0, unroll=True)

    def apply(i, c):
        sums[1 + i] = front(i)

        @pl.when(i == ITERS - 1)
        def _():
            packed = jnp.zeros((1, 128), F32)
            for k, n in enumerate((0, 1, 3, 2)):
                packed = jnp.where(lane1 == k, whole(sums[n]), packed)
            arsrc[0:1, :] = packed
            exchange(0, ar2, g2, member2)

        sums[3 + i] = back(i + 1)
        return c

    lax.fori_loop(0, ITERS, apply, 0)
    wait_bytes(ar2, arecv.at[0])
    arsrc[8:9, :] = arsrc[0:1, :] + jnp.sum(ar2[...], axis=0, keepdims=True)
    exchange(1, ar1, g1, member1)
    mask_sib().wait_send()

    @pl.when(sends_down)
    def _():
        mask_down(0).wait_send()
        mask_down(1).wait_send()

    @pl.when(sends_up)
    def _():
        mask_up(0).wait_send()
        mask_up(1).wait_send()

    def drain(l, c):
        part_sib(l).wait_send()

        @pl.when(sends_down)
        def _():
            part_down(l, 0).wait_send()
            part_down(l, 1).wait_send()

        @pl.when(sends_up)
        def _():
            part_up(l, 0).wait_send()
            part_up(l, 1).wait_send()

        for i in range(ITERS):

            @pl.when(has_prev)
            def _():
                halo_up(i, l).wait_send()

            @pl.when(has_next)
            def _():
                halo_down(i, l).wait_send()

        return c

    lax.fori_loop(0, lays, drain, 0)

    def landed(i):
        wait_bytes(fields.at[i, :, pl.ds(0, at * (2 * nl - 1))], trecv.at[i])
        src, dst = piece(i, 0, 0)
        pltpu.make_async_copy(src, dst, tlocal.at[i]).wait()
        wait_bytes(fields.at[i, :, pl.ds(0, at * (2 * nl - 1))], tsend.at[i])

    landed(0)
    landed(1)
    wait_bytes(ar2, asend.at[0])
    wait_bytes(ar1, arecv.at[1])
    total = arsrc[8:9, :] + jnp.sum(ar1[...], axis=0, keepdims=True)
    bb, e0, yy, e1 = (jnp.sum(jnp.where(lane1 == k, total, 0.0), axis=1, keepdims=True) for k in range(4))
    a0 = bb / e0
    rr = a0 * a0 * yy - bb
    beta = rr / bb
    grown = 1.0 + beta
    a1 = rr / (grown * grown * e0 - 2.0 * a0 * grown * yy + a0 * a0 * e1)
    k0_ref[...] = jnp.broadcast_to(a0 + a1 * grown, (1, 128))
    k1_ref[...] = jnp.broadcast_to(a0 * a1, (1, 128))

    landed(2)
    wait_bytes(ar1, asend.at[1])


def combine(fields, k0, k1, est, res):
    a, c = k0[...], k1[...]
    for r in range(fields.shape[1]):
        b, y1, y2 = fields[0, r], fields[1, r], fields[2, r]
        est[r] = a * b - c * y1
        res[r] = b - a * y1 + c * y2


def per_device(shape, measured_slopes, valid_mask, layer_offsets, reg_weight):
    nl, tiles = shape
    dirs, _, rows, cols = measured_slopes.shape
    lays = layer_offsets.shape[1]
    width = cols // (2 * nl)
    at = width // 128
    nt, st = at + 1, 2 * at + 2
    zs = 2 if tiles % 16 == 0 else 1
    g1, g2 = nl * zs * 2, tiles // (zs * 2)
    vm = lambda *s: pltpu.VMEM(s, F32)
    dma = lambda *s: pltpu.SemaphoreType.DMA(s)
    out = jax.ShapeDtypeStruct((3, rows, cols // 128, 128), F32)
    slopes = measured_slopes.reshape(dirs, 2, rows, cols // 128, 128).transpose(0, 2, 3, 1, 4)
    slopes = slopes.reshape(dirs, rows, cols // 64, 128)
    fields, k0, k1 = pl.pallas_call(
        functools.partial(kernel, (dirs, lays, tiles, rows, cols, nl)),
        out_shape=(out,) + (jax.ShapeDtypeStruct((1, 128), F32),) * 2,
        in_specs=[pl.BlockSpec(memory_space=pltpu.HBM)] * 2 + [pl.BlockSpec(memory_space=pltpu.SMEM)] * 2,
        out_specs=(pl.BlockSpec(memory_space=pltpu.HBM),) + (pl.BlockSpec(memory_space=pltpu.VMEM),) * 2,
        scratch_shapes=[
            vm(dirs, 2 * st, rows + 4, 128),
            pltpu.VMEM((rows, 128 * st), jnp.int32),
            vm(2, st, 24, 128),
            vm(dirs, st, 48, 128),
            vm(2, lays, nt, 40, 128),
            vm(lays, nt, 40, 128),
            vm(lays, nt, 16, 128),
            vm(lays, nt, 8, 128),
            vm(2, nt, 16, 128),
            vm(nt, 56, 128),
            vm(3, lays, nt, 72, 128),
            vm(lays, nt, 72, 128),
            vm(5, 8, 128),
            vm(2, nt, 48, 128),
            vm(dirs, nt, 40, 128),
            vm(lays, nt, 32, 128),
            vm(3, lays, at * 2 * rows, 128),
            vm(16, 128),
            vm(g1 - 1, 128),
            vm(g2 - 1, 128),
            dma(2), dma(3), dma(3), dma(lays, 3), dma(lays, 3), dma(2, lays, 2), dma(2, lays, 2),
            dma(3), dma(3), dma(3), dma(2), dma(2),
        ],
        compiler_params=pltpu.CompilerParams(
            collective_id=0, has_side_effects=True, vmem_limit_bytes=56 * 1024 * 1024
        ),
    )(slopes, valid_mask, layer_offsets.transpose(1, 2, 0), reg_weight)
    part = jax.ShapeDtypeStruct((rows, cols // 128, 128), F32)
    whole = pl.BlockSpec(memory_space=pltpu.VMEM)
    est, res = pl.pallas_call(
        combine, out_shape=(part, part), in_specs=[whole] * 3, out_specs=(whole, whole)
    )(fields, k0, k1)
    return est.reshape(1, rows, cols), res.reshape(1, rows, cols)


def solution(mesh):
    return jax.shard_map(
        functools.partial(per_device, (mesh.shape["layer"], mesh.shape["tile"])),
        mesh=mesh,
        in_specs=(P(None, None, "tile", None), P("tile", None), P(), P()),
        out_specs=(P("layer", "tile", None), P("layer", "tile", None)),
        check_vma=False,
    )
```

```python
import functools

import jax
import jax.numpy as jnp
from jax import lax
from jax.experimental import pallas as pl
from jax.experimental.pallas import tpu as pltpu
from jax.sharding import PartitionSpec as P

MESH = pl.DeviceIdType.MESH
F32 = jnp.float32
HALO = 8
MARGIN = 64
ITERS = 2
REACH = 17


def kernel(
    cfg,
    slopes_hbm, mask_hbm, off, reg,
    fields, k0_ref, k1_ref,
    sl, mki, eb, q0, cb, sib, prv, nxt, ms, mb, xb, xw, sums, pb, qb, lb, ya, arsrc, ar1, ar2,
    in_sem, msend, mrecv, csend, crecv, hsend, hrecv, tsend, trecv, tlocal, asend, arecv,
):
    dirs, lays, tiles, rows, cols, nl = cfg
    two = 2 * rows
    width = cols // (2 * nl)
    at = width // 128
    nt = at + 1
    st = 2 * at + 2
    zs, xs = (2, 4) if tiles % 16 == 0 else (1, tiles // 2)
    g1 = nl * zs * 2
    g2 = tiles // (zs * 2)
    lay = lax.axis_index("layer")
    t = lax.axis_index("tile")
    chip = lax.div(t, 2)
    h = lax.rem(t, 2)
    chips = tiles // 2
    has_prev = chip > 0
    has_next = chip < chips - 1
    prev0 = 2 * chip - 2
    next0 = 2 * chip + 2
    lane = lax.broadcasted_iota(jnp.int32, (8, 128), 1)
    sub = lax.broadcasted_iota(jnp.int32, (8, 128), 0)
    zero = jnp.zeros((8, 128), F32)

    def rdma(src, dst, ss, rs, dev):
        return pltpu.make_async_remote_copy(
            src_ref=src, dst_ref=dst, send_sem=ss, recv_sem=rs, device_id=dev, device_id_type=MESH
        )

    def wait_bytes(ref, sem):
        pltpu.make_async_copy(ref, ref, sem).wait()

    barrier = pltpu.get_barrier_semaphore()

    def greet(dev):
        pl.semaphore_signal(barrier, inc=1, device_id=dev, device_id_type=MESH)

    other = 2 * chip + 1 - h

    @pl.when(has_prev)
    def _():
        greet((lay, prev0))
        greet((lay, prev0 + 1))

    @pl.when(has_next)
    def _():
        greet((lay, next0))
        greet((lay, next0 + 1))

    tx, tz, ty = lax.rem(chip, xs), lax.rem(lax.div(chip, xs), zs), lax.div(chip, xs * zs)
    me1 = (lay * zs + tz) * 2 + h
    me2 = ty * xs + tx

    def tile_at(y, z, x, core):
        return ((y * zs + z) * xs + x) * 2 + core

    def member1(d):
        index = lax.rem(me1 + d, g1)
        there = lax.div(index, 2 * zs)
        return (there, tile_at(ty, lax.rem(lax.div(index, 2), zs), tx, lax.rem(index, 2)))

    def member2(d):
        index = lax.rem(me2 + d, g2)
        return (lay, tile_at(lax.div(index, xs), tz, lax.rem(index, xs), h))

    def greet1(d, c):
        greet(member1(d))
        return c

    def greet2(d, c):
        greet(member2(d))
        return c

    lax.fori_loop(1, g1, greet1, 0, unroll=True)
    lax.fori_loop(1, g2, greet2, 0, unroll=True)

    span = 2 * width

    def mask_in(first, count, at_tile):
        src, dst = pl.ds(pl.multiple_of(first, 128), count), pl.ds(128 * at_tile, count)
        return pltpu.make_async_copy(mask_hbm.at[:, src], mki.at[:, dst], in_sem.at[0])

    def slopes_in(first, count, at_tile):
        src, dst = pl.ds(lax.div(first, 64), count // 64), pl.ds(2 * at_tile, count // 64)

        def one(i, c):
            pltpu.make_async_copy(slopes_hbm.at[:, i, src], sl.at[:, dst, i], in_sem.at[1]).start()
            return c

        lax.fori_loop(0, rows, one, 0)

    def slopes_wait(first, count, at_tile):
        dst = sl.at[:, pl.ds(2 * at_tile, count // 64), pl.ds(0, rows)]
        pltpu.make_async_copy(dst, dst, in_sem.at[1]).wait()

    def cases(act):
        @pl.when(lay == 0)
        def _():
            act(0, span + 128, 1)

        @pl.when(lay == nl - 1)
        def _():
            act(span * (nl - 1) - 128, span + 128, 0)

        @pl.when((lay > 0) & (lay < nl - 1))
        def _():
            act(span * lay - 128, span + 256, 0)

    cases(lambda *w: mask_in(*w).start())
    cases(slopes_in)

    @pl.when(lay == 0)
    def _():
        mki[:, 0:128] = jnp.zeros((rows, 128), jnp.int32)
        sl[:, 0:2, 0:rows] = jnp.zeros((dirs, 2, rows, 128), F32)

    @pl.when(lay == nl - 1)
    def _():
        mki[:, 128 * (st - 1) :] = jnp.zeros((rows, 128), jnp.int32)
        sl[:, 2 * st - 2 :, 0:rows] = jnp.zeros((dirs, 2, rows, 128), F32)

    sib[:, :, 0:8] = jnp.zeros((lays, nt, 8, 128), F32)
    sib[:, :, rows + 25 : 40] = jnp.zeros((lays, nt, 15 - rows, 128), F32)
    prv[:, :, HALO + 1 : 16] = jnp.zeros((lays, nt, 15 - HALO, 128), F32)
    mb[:, HALO + 1 + two + HALO : 56] = jnp.zeros((nt, 56 - two - 2 * HALO - 1, 128), F32)

    @pl.when(jnp.logical_not(has_prev))
    def _():
        prv[:, :, 0 : HALO + 1] = jnp.zeros((lays, nt, HALO + 1, 128), F32)
        mb[:, 0 : HALO + 1] = jnp.zeros((nt, HALO + 1, 128), F32)
        xb[0:2, :, :, 0:24] = jnp.zeros((2, lays, nt, 24, 128), F32)

    @pl.when(jnp.logical_not(has_next))
    def _():
        nxt[...] = jnp.zeros_like(nxt)
        mb[:, HALO + 1 + two : HALO + 1 + two + HALO] = jnp.zeros((nt, HALO, 128), F32)
        xb[0:2, :, :, 24 + two :] = jnp.zeros((2, lays, nt, 48 - two, 128), F32)

    eb[:, :, 0:8] = jnp.zeros((2, st, 8, 128), F32)
    eb[:, :, 16:24] = jnp.zeros((2, st, 8, 128), F32)
    q0[:, :, 0:16] = jnp.zeros((dirs, st, 16, 128), F32)
    q0[:, :, 32:48] = jnp.zeros((dirs, st, 16, 128), F32)
    cb[:, :, :, 0:8, :] = jnp.zeros((2, lays, nt, 8, 128), F32)

    cases(lambda *w: mask_in(*w).wait())
    bands = [slice(0, 8), slice(8, rows)]
    for k in range(2):
        for band in bands:
            turned = [
                pltpu.roll(mki[band, 128 * j : 128 * j + 128].astype(F32), MARGIN + HALO, 1)
                for j in range(at * k, at * k + nt + 1)
            ]
            keep = lane[: band.stop - band.start] < MARGIN + HALO
            for j in range(nt):
                ms[k, j, band, :] = jnp.where(keep, turned[j], turned[j + 1])
    mine = HALO + 1 + rows * h
    for j in range(nt):
        mb[j, pl.ds(mine, rows), :] = ms[h, j, 0:rows, :]
    def mask_sib():
        return rdma(
            ms.at[1 - h, :, pl.ds(0, rows)], mb.at[:, pl.ds(mine, rows)], msend.at[0], mrecv.at[0], (lay, other)
        )

    def mask_down(k):
        return rdma(
            ms.at[k, :, pl.ds(rows - HALO - 1, HALO + 1)], mb.at[:, pl.ds(0, HALO + 1)],
            msend.at[1 + k], mrecv.at[1], (lay, next0 + k),
        )

    def mask_up(k):
        return rdma(
            ms.at[k, :, pl.ds(0, HALO)], mb.at[:, pl.ds(HALO + 1 + two, HALO)],
            msend.at[1 + k], mrecv.at[2], (lay, prev0 + k),
        )

    sends_down = has_next & (h == 1)
    sends_up = has_prev & (h == 0)
    cases(slopes_wait)
    first_row = rows * t

    def own_adjoint(g, c):
        for band in bands:
            for j in range(st):
                at_cols = slice(128 * j, 128 * j + 128)
                m = mki[band, at_cols].astype(F32)
                u = m * sl[g, 2 * j, band, :]
                w = m * sl[g, 2 * j + 1, band, :]
                eb[0, j, 8 + band.start : 8 + band.stop, :] = u + w
                eb[1, j, 8 + band.start : 8 + band.stop, :] = u - w
        for rb in range(2):
            lo, up = 8 + 8 * rb, 7 + 8 * rb
            row_in = (first_row + 8 * rb + sub < rows * tiles).astype(F32)
            right = []
            for j in range(st):
                right.append(pltpu.roll(eb[0, j, up : up + 8, :] + eb[1, j, lo : lo + 8, :], 1, 1))
            for j in range(st):
                f = jnp.where(lane >= 1, right[j], right[max(j - 1, 0)])
                q = 0.5 * (f - eb[0, j, lo : lo + 8, :] - eb[1, j, up : up + 8, :])
                col_in = (span * lay - 128 + 128 * j + lane < cols).astype(F32)
                q0[g, j, 16 + 8 * rb : 24 + 8 * rb, :] = q * (row_in * col_in)
        return c

    lax.fori_loop(0, dirs, own_adjoint, 0)
    pl.semaphore_wait(
        barrier,
        2 * has_prev.astype(jnp.int32) + 2 * has_next.astype(jnp.int32) + (g1 - 1) + (g2 - 1),
    )

    mask_sib().start()

    @pl.when(sends_down)
    def _():
        mask_down(0).start()
        mask_down(1).start()

    @pl.when(sends_up)
    def _():
        mask_up(0).start()
        mask_up(1).start()


    def part_sib(l):
        return rdma(
            cb.at[1 - h, l, :, pl.ds(8, rows + 17)], sib.at[l, :, pl.ds(8, rows + 17)],
            csend.at[l, 0], crecv.at[l, 0], (lay, other),
        )

    def part_down(l, k):
        return rdma(
            cb.at[k, l, :, pl.ds(16 + rows, 9)], prv.at[l, :, pl.ds(0, 9)],
            csend.at[l, 1 + k], crecv.at[l, 1], (lay, next0 + k),
        )

    def part_up(l, k):
        return rdma(
            cb.at[k, l, :, pl.ds(8, 8)], nxt.at[l], csend.at[l, 1 + k], crecv.at[l, 2], (lay, prev0 + k)
        )

    def blocks(l, first):
        for k8 in range(2):
            at8 = pl.multiple_of(8 * (first + k8), 8)
            total = [[zero] * nt, [zero] * nt]
            for g in range(dirs):
                a, s = off[l, 0, g], MARGIN + off[l, 1, g]
                start = 8 + at8 - a
                turned = [pltpu.roll(q0[g, j, pl.ds(start, 8), :], s, 1) for j in range(st)]
                keep = lane < s
                for k in range(2):
                    for j in range(nt):
                        total[k][j] = total[k][j] + jnp.where(keep, turned[at * k + j], turned[at * k + j + 1])
            for k in range(2):
                for j in range(nt):
                    cb[k, l, j, pl.ds(8 + at8, 8), :] = total[k][j]

    def parts(step, c):
        l, last = lax.rem(step, lays), lax.div(step, lays)
        blocks(l, 2 * lax.rem(h + last, 2))

        @pl.when((last == 0) & sends_down)
        def _():
            part_down(l, 0).start()
            part_down(l, 1).start()

        @pl.when((last == 0) & sends_up)
        def _():
            part_up(l, 0).start()
            part_up(l, 1).start()

        @pl.when(last == 1)
        def _():
            part_sib(l).start()

        return c

    lax.fori_loop(0, 2 * lays, parts, 0)

    c0 = width * (2 * lay + h)
    xcol = [c0 - MARGIN + 128 * j + lane for j in range(nt)]
    x_in = [((v >= 0) & (v < cols)).astype(F32) for v in xcol]
    x_own = [((v >= c0) & (v < c0 + width)).astype(F32) for v in xcol]
    pcol = [c0 - MARGIN - HALO + 128 * j + lane for j in range(nt)]
    p_in = [((v >= 0) & (v < cols)).astype(F32) for v in pcol]
    p_own = [((v >= c0) & (v < c0 + width)).astype(F32) for v in pcol]
    chip_row = two * chip

    def row_inside(start):
        r = chip_row + start + sub
        return ((r >= 0) & (r < rows * tiles)).astype(F32)

    def halo_up(i, l):
        return rdma(
            xb.at[i, l, :, pl.ds(24, REACH)], xb.at[i, l, :, pl.ds(24 + two, REACH)],
            hsend.at[i, l, 0], hrecv.at[i, l, 0], (lay, prev0 + h),
        )

    def halo_down(i, l):
        return rdma(
            xb.at[i, l, :, pl.ds(24 + two - REACH, REACH)], xb.at[i, l, :, pl.ds(24 - REACH, REACH)],
            hsend.at[i, l, 1], hrecv.at[i, l, 1], (lay, next0 + h),
        )

    def send_halo(i, l):
        @pl.when(has_prev)
        def _():
            halo_up(i, l).start()

        @pl.when(has_next)
        def _():
            halo_down(i, l).start()

    def wait_halo(i, l):
        @pl.when(has_prev)
        def _():
            halo_down(i, l).wait_recv()

        @pl.when(has_next)
        def _():
            halo_up(i, l).wait_recv()

    def piece(i, l, half):
        src = ya.at[i, l, pl.ds(at * rows * half, at * rows)].reshape(rows, at, 128)
        dst = fields.at[i, :, pl.ds(at * (2 * lay + h), at)]
        return src, dst

    def send_pieces(i, l):
        for half in range(2):
            src, dst = piece(i, l, half)
            here = (l == lay) & (half == h)

            @pl.when(here)
            def _():
                pltpu.make_async_copy(src, dst, tlocal.at[i]).start()

            @pl.when(jnp.logical_not(here))
            def _():
                rdma(src, dst, tsend.at[i], trecv.at[i], (l, 2 * chip + half)).start()

    def stage(i, l, rb, value):
        turned = [pltpu.roll(v, MARGIN, 1) for v in value]
        for k in range(at):
            ya[i, l, pl.ds(at * 8 * rb + k, 8, stride=at), :] = jnp.where(lane < MARGIN, turned[k], turned[k + 1])

    def finish_b(l, acc):
        part_sib(l).wait_recv()

        @pl.when(has_prev)
        def _():
            part_down(l, 0).wait_recv()

        @pl.when(has_next)
        def _():
            part_up(l, 0).wait_recv()

        for rb in range(two // 8):
            value = []
            for j in range(nt):
                v = cb[h, l, j, pl.ds(16 + 8 * rb - rows * h, 8), :]
                v = v + sib[l, j, pl.ds(16 + 8 * rb - rows * (1 - h), 8), :]
                if rb < 2:
                    v = v + prv[l, j, 8 * rb : 8 * rb + 8, :]
                if rb == two // 8 - 1:
                    v = v + nxt[l, j]
                v = v * x_in[j]
                acc = acc + x_own[j] * (v * v)
                xb[0, l, j, 24 + 8 * rb : 32 + 8 * rb, :] = v
                value.append(v)
            stage(0, l, rb, value)
        send_halo(0, l)
        return acc

    sums[0] = lax.fori_loop(0, lays, finish_b, zero)

    mask_sib().wait_recv()

    @pl.when(has_prev)
    def _():
        mask_down(0).wait_recv()

    @pl.when(has_next)
    def _():
        mask_up(0).wait_recv()

    def beside(value):
        n = len(value)
        r = [pltpu.roll(v, 1, 1) for v in value]
        l = [pltpu.roll(v, 127, 1) for v in value]
        left = [jnp.where(lane >= 1, r[j], r[(j - 1) % n]) for j in range(n)]
        right = [jnp.where(lane < 127, l[j], l[(j + 1) % n]) for j in range(n)]
        return left, right

    def front(i):
        def smooth(l, acc):
            wait_halo(i, l)

            @pl.when(l >= lays // 2)
            def _():
                send_pieces(i, l - lays // 2)

            for j in range(nt):
                xw[l, j] = xb[i, l, j]
            part = zero
            for rb in range(4):
                row = -1 + 8 * rb
                mid = [xb[i, l, j, 24 + row : 32 + row, :] for j in range(nt)]
                left, right = beside(mid)
                inside = row_inside(row)
                own = ((row + sub >= 0) & (row + sub < two)).astype(F32)
                for j in range(nt):
                    v = 4.0 * mid[j] - xb[i, l, j, 23 + row : 31 + row, :] - xb[i, l, j, 25 + row : 33 + row, :]
                    v = (v - left[j] - right[j]) * (inside * x_in[j])
                    lb[l, j, 8 * rb : 8 * rb + 8, :] = v
                    part = part + (own * x_own[j]) * (v * v)
            return acc + reg[l] * part

        energy = lax.fori_loop(0, lays, smooth, zero)

        def give(l, c):
            send_pieces(i, l)
            return c

        lax.fori_loop(lays // 2, lays, give, 0)

        def project(g, acc):
            for rb in range(6):
                total = [zero] * nt
                for l in range(lays):
                    a, s = off[l, 0, g], HALO - off[l, 1, g]
                    start = 15 + 8 * rb + a
                    turned = [pltpu.roll(xw[l, j, pl.ds(start, 8), :], s, 1) for j in range(nt)]
                    keep = lane >= s
                    total = [total[j] + jnp.where(keep, turned[j], turned[(j - 1) % nt]) for j in range(nt)]
                inside = row_inside(8 * rb - 9)
                total = [total[j] * (inside * p_in[j]) for j in range(nt)]
                turned = [pltpu.roll(v, 127, 1) for v in total]
                for j in range(nt):
                    pb[0, j, 8 * rb : 8 * rb + 8, :] = total[j]
                    pb[1, j, 8 * rb : 8 * rb + 8, :] = jnp.where(lane < 127, turned[j], turned[(j + 1) % nt])
            for rb in range(5):
                up, lo, dn = 8 * rb, 8 * rb + 1, 8 * rb + 2
                turned, rest = [], []
                inside = row_inside(8 * rb - 8)
                for j in range(nt):
                    m_lo, m_up = mb[j, lo : lo + 8, :], mb[j, up : up + 8, :]
                    p_lo, r_lo = pb[0, j, lo : lo + 8, :], pb[1, j, lo : lo + 8, :]
                    e1 = m_lo * (pb[1, j, dn : dn + 8, :] - p_lo)
                    e2 = m_lo * (r_lo - pb[0, j, dn : dn + 8, :])
                    e1_up = m_up * (r_lo - pb[0, j, up : up + 8, :])
                    e2_up = m_up * (pb[1, j, up : up + 8, :] - p_lo)
                    if 1 <= rb <= two // 8:
                        acc = acc + (0.5 * p_own[j]) * (e1 * e1 + e2 * e2)
                    turned.append(pltpu.roll(e1_up + e2, 1, 1))
                    rest.append(e1 + e2_up)
                for j in range(nt):
                    f = jnp.where(lane >= 1, turned[j], turned[(j - 1) % nt])
                    qb[g, j, 8 * rb : 8 * rb + 8, :] = (f - rest[j]) * (0.5 * inside * p_in[j])
            return acc

        return lax.fori_loop(0, dirs, project, energy)

    def back(i):
        def layer(l, acc):
            for rb in range(two // 8):
                total = [zero] * nt
                for g in range(dirs):
                    a, s = off[l, 0, g], lax.rem(120 + off[l, 1, g], 128)
                    start = 8 + 8 * rb - a
                    turned = [pltpu.roll(qb[g, j, pl.ds(start, 8), :], s, 1) for j in range(nt)]
                    keep = lane < 120 + off[l, 1, g]
                    total = [total[j] + jnp.where(keep, turned[j], turned[(j + 1) % nt]) for j in range(nt)]
                lo = 8 * rb + 1
                mid = [lb[l, j, lo : lo + 8, :] for j in range(nt)]
                left, right = beside(mid)
                value = []
                for j in range(nt):
                    v = 4.0 * mid[j] - lb[l, j, lo - 1 : lo + 7, :] - lb[l, j, lo + 1 : lo + 9, :] - left[j] - right[j]
                    v = (total[j] + reg[l] * v) * x_in[j]
                    acc = acc + x_own[j] * (v * v)
                    xb[i, l, j, 24 + 8 * rb : 32 + 8 * rb, :] = v
                    value.append(v)
                stage(i, l, rb, value)

            @pl.when(i < ITERS)
            def _():
                send_halo(i, l)

            @pl.when(i == ITERS)
            def _():
                send_pieces(i, l)

            return acc

        return lax.fori_loop(0, lays, layer, zero)

    lane1 = lane[0:1]

    def whole(v):
        return jnp.sum(jnp.sum(v, axis=0, keepdims=True), axis=1, keepdims=True)

    def exchange(stage_id, slots, count, member):
        def one(d, c):
            rdma(
                arsrc.at[pl.ds(8 * stage_id, 1)], slots.at[pl.ds(count - 1 - d, 1)],
                asend.at[stage_id], arecv.at[stage_id], member(d),
            ).start()
            return c

        lax.fori_loop(1, count, one, 0, unroll=True)

    def apply(i, c):
        sums[1 + i] = front(i)

        @pl.when(i == ITERS - 1)
        def _():
            packed = jnp.zeros((1, 128), F32)
            for k, n in enumerate((0, 1, 3, 2)):
                packed = jnp.where(lane1 == k, whole(sums[n]), packed)
            arsrc[0:1, :] = packed
            exchange(0, ar2, g2, member2)

        sums[3 + i] = back(i + 1)
        return c

    lax.fori_loop(0, ITERS, apply, 0)
    wait_bytes(ar2, arecv.at[0])
    arsrc[8:9, :] = arsrc[0:1, :] + jnp.sum(ar2[...], axis=0, keepdims=True)
    exchange(1, ar1, g1, member1)
    mask_sib().wait_send()

    @pl.when(sends_down)
    def _():
        mask_down(0).wait_send()
        mask_down(1).wait_send()

    @pl.when(sends_up)
    def _():
        mask_up(0).wait_send()
        mask_up(1).wait_send()

    def drain(l, c):
        part_sib(l).wait_send()

        @pl.when(sends_down)
        def _():
            part_down(l, 0).wait_send()
            part_down(l, 1).wait_send()

        @pl.when(sends_up)
        def _():
            part_up(l, 0).wait_send()
            part_up(l, 1).wait_send()

        for i in range(ITERS):

            @pl.when(has_prev)
            def _():
                halo_up(i, l).wait_send()

            @pl.when(has_next)
            def _():
                halo_down(i, l).wait_send()

        return c

    lax.fori_loop(0, lays, drain, 0)

    def landed(i):
        wait_bytes(fields.at[i, :, pl.ds(0, at * (2 * nl - 1))], trecv.at[i])
        src, dst = piece(i, 0, 0)
        pltpu.make_async_copy(src, dst, tlocal.at[i]).wait()
        wait_bytes(fields.at[i, :, pl.ds(0, at * (2 * nl - 1))], tsend.at[i])

    landed(0)
    landed(1)
    wait_bytes(ar2, asend.at[0])
    wait_bytes(ar1, arecv.at[1])
    total = arsrc[8:9, :] + jnp.sum(ar1[...], axis=0, keepdims=True)
    bb, e0, yy, e1 = (jnp.sum(jnp.where(lane1 == k, total, 0.0), axis=1, keepdims=True) for k in range(4))
    a0 = bb / e0
    rr = a0 * a0 * yy - bb
    beta = rr / bb
    grown = 1.0 + beta
    a1 = rr / (grown * grown * e0 - 2.0 * a0 * grown * yy + a0 * a0 * e1)
    k0_ref[...] = jnp.broadcast_to(a0 + a1 * grown, (1, 128))
    k1_ref[...] = jnp.broadcast_to(a0 * a1, (1, 128))

    landed(2)
    wait_bytes(ar1, asend.at[1])


def combine(fields, k0, k1, est, res):
    a, c = k0[...], k1[...]
    for r in range(fields.shape[1]):
        b, y1, y2 = fields[0, r], fields[1, r], fields[2, r]
        est[r] = a * b - c * y1
        res[r] = b - a * y1 + c * y2


def per_device(shape, measured_slopes, valid_mask, layer_offsets, reg_weight):
    nl, tiles = shape
    dirs, _, rows, cols = measured_slopes.shape
    lays = layer_offsets.shape[1]
    width = cols // (2 * nl)
    at = width // 128
    nt, st = at + 1, 2 * at + 2
    zs = 2 if tiles % 16 == 0 else 1
    g1, g2 = nl * zs * 2, tiles // (zs * 2)
    vm = lambda *s: pltpu.VMEM(s, F32)
    dma = lambda *s: pltpu.SemaphoreType.DMA(s)
    out = jax.ShapeDtypeStruct((3, rows, cols // 128, 128), F32)
    slopes = measured_slopes.reshape(dirs, 2, rows, cols // 128, 128).transpose(0, 2, 3, 1, 4)
    slopes = slopes.reshape(dirs, rows, cols // 64, 128)
    fields, k0, k1 = pl.pallas_call(
        functools.partial(kernel, (dirs, lays, tiles, rows, cols, nl)),
        out_shape=(out,) + (jax.ShapeDtypeStruct((1, 128), F32),) * 2,
        in_specs=[pl.BlockSpec(memory_space=pltpu.HBM)] * 2 + [pl.BlockSpec(memory_space=pltpu.SMEM)] * 2,
        out_specs=(pl.BlockSpec(memory_space=pltpu.HBM),) + (pl.BlockSpec(memory_space=pltpu.VMEM),) * 2,
        scratch_shapes=[
            vm(dirs, 2 * st, rows + 4, 128),
            pltpu.VMEM((rows, 128 * st), jnp.int32),
            vm(2, st, 24, 128),
            vm(dirs, st, 48, 128),
            vm(2, lays, nt, 40, 128),
            vm(lays, nt, 48, 128),
            vm(lays, nt, 24, 128),
            vm(lays, nt, 8, 128),
            vm(2, nt, 16, 128),
            vm(nt, 64, 128),
            vm(3, lays, nt, 72, 128),
            vm(lays, nt, 72, 128),
            vm(5, 8, 128),
            vm(2, nt, 48, 128),
            vm(dirs, nt, 40, 128),
            vm(lays, nt, 32, 128),
            vm(3, lays, at * 2 * rows, 128),
            vm(16, 128),
            vm(g1 - 1, 128),
            vm(g2 - 1, 128),
            dma(2), dma(3), dma(3), dma(lays, 3), dma(lays, 3), dma(2, lays, 2), dma(2, lays, 2),
            dma(3), dma(3), dma(3), dma(2), dma(2),
        ],
        compiler_params=pltpu.CompilerParams(
            collective_id=0, has_side_effects=True, vmem_limit_bytes=56 * 1024 * 1024
        ),
    )(slopes, valid_mask, layer_offsets.transpose(1, 2, 0), reg_weight)
    part = jax.ShapeDtypeStruct((rows, cols // 128, 128), F32)
    whole = pl.BlockSpec(memory_space=pltpu.VMEM)
    est, res = pl.pallas_call(
        combine, out_shape=(part, part), in_specs=[whole] * 3, out_specs=(whole, whole)
    )(fields, k0, k1)
    return est.reshape(1, rows, cols), res.reshape(1, rows, cols)


def solution(mesh):
    return jax.shard_map(
        functools.partial(per_device, (mesh.shape["layer"], mesh.shape["tile"])),
        mesh=mesh,
        in_specs=(P(None, None, "tile", None), P("tile", None), P(), P()),
        out_specs=(P("layer", "tile", None), P("layer", "tile", None)),
        check_vma=False,
    )
```
